512 devices in a mesh: row: 64 (over x, z), col: 8 (over y, core).
Axes of the slice: x: 4, y: 4, z: 16, core: 2. Of those that a mesh axis runs over, the one named last changes fastest.
Arguments:
- momentum: float32 [8192, 26624], P('row', 'col')
- gradient: bfloat16 [8192, 26624], P('row', 'col'), may hold values from -6 to 6
- factor: float32 [26624, 256], P(('col', 'row'))
Outputs:
- momentum_out: float32 [8192, 26624], P('row', 'col')
- weight_update: bfloat16 [8192, 26624], P('row', 'col')
- factor_out: float32 [26624, 256], P(('col', 'row'))
The draws below stay inside these ranges and needn't reach their ends.
All inputs are finite; a program needn't handle non-finite values.
Results may differ from the reference program's by a relative error of at most 0.0013.
Values sent between devices are 32-bit elements; how exact they have to be, the bound alone decides.
A program may use at most 64 MiB of HBM per device.

```python
import math
import jax
import jax.numpy as jnp
from jax import lax

R = 256
N_COLS = 26624
M_ROWS = 8192


def draw_momentum(key, part):
    key = jax.random.fold_in(key, 7)
    base_key, row_key, col_key = jax.random.split(key, 3)
    row_ramp = 3.0 ** (jnp.arange(M_ROWS, dtype=jnp.float32) / (M_ROWS - 1))
    row_scale = row_ramp * jnp.exp(jax.random.uniform(row_key, (M_ROWS,), jnp.float32, math.log(0.4), math.log(4.0)))
    col_scale = jnp.exp(jax.random.uniform(col_key, (N_COLS,), jnp.float32, math.log(0.4), math.log(4.0)))
    entries = jax.random.truncated_normal(base_key, -6.0, 6.0, (M_ROWS, N_COLS), jnp.float32)
    return (0.5 * entries * row_scale[:, None] * col_scale[None, :]).astype(jnp.float32)


def draw_factor(key, part):
    key = jax.random.fold_in(key, 11)
    shared_key, gain_key, sign_key, noise_key = jax.random.split(key, 4)
    shared = 0.3 * jax.random.truncated_normal(shared_key, -6.0, 6.0, (N_COLS, 1), jnp.float32)
    noise = jax.random.truncated_normal(noise_key, -6.0, 6.0, (N_COLS, R), jnp.float32)
    gains = jnp.exp(jax.random.uniform(gain_key, (R,), jnp.float32, math.log(0.5), math.log(2.0)))
    signs = (2 * jax.random.randint(sign_key, (R,), 0, 2) - 1).astype(jnp.float32)
    return ((shared * signs[None, :] + noise) * gains[None, :]).astype(jnp.float32)


def levels(own_key, shape, cuts, low, largest):
    level = 1.0
    for position, shards_of in cuts:
        draws = jax.random.uniform(jax.random.fold_in(jax.random.fold_in(own_key, 6), position), (shards_of,), jnp.float32, low / len(cuts), largest / len(cuts))
        level = level * jnp.repeat(jnp.exp(draws), shape[position] // shards_of).reshape((-1,) + (1,) * (len(shape) - 1 - position))
    return level


def bell_draw(key, dims, spread, limit, pieces=(), kind=jnp.bfloat16):
    array = spread * jax.random.normal(key, dims, jnp.float32)
    if pieces:
        array = array * levels(key, dims, pieces, -0.22, 0.18)
    return jnp.clip(array, -limit, limit).astype(kind)


def setup_inputs(seed: int = 0) -> dict:
    keys = jax.random.split(jax.random.key(seed), 4)
    return {
        "momentum": draw_momentum(jax.random.fold_in(keys[3], 71), 0),
        "gradient": bell_draw(keys[1], (M_ROWS, N_COLS), 1.0, 6.0, ((0, 64), (1, 8))),
        "factor": draw_factor(jax.random.fold_in(keys[3], 71), 0),
    }


HIGHEST = lax.Precision.HIGHEST
MOMENTUM_KEEP = 0.8
STEP_SIZE = 0.3
EPSILON = 1e-06

def unit_columns(left_panel, gram_matrix):
    lower_factor = jnp.linalg.cholesky(gram_matrix)
    return lax.linalg.triangular_solve(lower_factor, left_panel, left_side=False, lower=True, transpose_a=True)

def reference(momentum, gradient, factor):
    buffer = momentum + gradient.astype(jnp.float32)
    left_panel = jnp.dot(buffer.astype(jnp.float32), factor.astype(jnp.float32), precision=HIGHEST, preferred_element_type=jnp.float32)
    gram_matrix = jnp.dot(left_panel.T.astype(jnp.float32), left_panel.astype(jnp.float32), precision=HIGHEST, preferred_element_type=jnp.float32)
    left_basis = unit_columns(left_panel, gram_matrix)
    right_factor = jnp.dot(buffer.T.astype(jnp.float32), left_basis.astype(jnp.float32), precision=HIGHEST, preferred_element_type=jnp.float32)
    momentum_out = buffer - (1.0 - MOMENTUM_KEEP) * jnp.dot(left_basis.astype(jnp.float32), right_factor.T.astype(jnp.float32), precision=HIGHEST, preferred_element_type=jnp.float32)
    column_rms = jnp.sqrt(lax.optimization_barrier(jnp.sum(right_factor * right_factor, axis=0)) / N_COLS + EPSILON)
    factor_out = right_factor / column_rms
    update = jnp.dot(left_basis.astype(jnp.float32), factor_out.T.astype(jnp.float32), precision=HIGHEST, preferred_element_type=jnp.float32)
    weight_update = (-STEP_SIZE * math.sqrt(M_ROWS / R) * update).astype(jnp.bfloat16)
    return (momentum_out, weight_update, factor_out)
```

```python
import functools
import math

import jax
import jax.numpy as jnp
from jax import lax
from jax.experimental import pallas as pl
from jax.experimental.pallas import tpu as pltpu
from jax.sharding import PartitionSpec as P

HIGHEST = lax.Precision.HIGHEST
MOMENTUM_KEEP = 0.8
STEP_SIZE = 0.3
EPSILON = 1e-06
F32 = jnp.float32
BF16 = jnp.bfloat16

NX, NZ = 4, 16
NC = 8
CH = 104
CA = 64
CB = CH - CA
ROWS, COLS, RANK = 128, 3328, 256
BLK = 256
NBLK = COLS // BLK
NB = 32


def split(value):
    high = value.astype(BF16)
    return high, (value - high.astype(F32)).astype(BF16)


def dot(a, b, dims=((1,), (0,))):
    return lax.dot_general(a, b, (dims, ((), ())), preferred_element_type=F32)


def dot3(a, b, dims=((1,), (0,))):
    return dot(a[0], b[0], dims) + (dot(a[0], b[1], dims) + dot(a[1], b[0], dims))


def dot6(a, b, dims=((1,), (0,))):
    return lax.dot_general(a, b, (dims, ((), ())), precision=HIGHEST, preferred_element_type=F32)


class Links:
    def __init__(self, ssem, rsem):
        self.ssem, self.rsem = ssem, rsem
        self.r, self.c = lax.axis_index("row"), lax.axis_index("col")
        self.x, self.z = self.r // NZ, self.r % NZ

    def mod(self, value, n):
        return lax.rem(value + 4 * n, n)

    def at_x(self, d):
        return {"row": self.mod(self.x + d, NX) * NZ + self.z, "col": self.c}

    def at_z(self, d):
        return {"row": self.x * NZ + self.mod(self.z + d, NZ), "col": self.c}

    def at_c(self, d):
        return {"row": self.r, "col": self.mod(self.c + d, NC)}

    def at_q(self, d):
        return {"row": self.x * NZ + (self.z // 4) * 4 + lax.rem(self.z + d, 4), "col": self.c}

    def copy(self, src, dst, recv, device, slot=0):
        return pltpu.make_async_remote_copy(
            src_ref=src, dst_ref=dst, send_sem=self.ssem.at[slot], recv_sem=recv,
            device_id=device, device_id_type=pl.DeviceIdType.MESH)

    def send(self, src, dst, recv, device, slot):
        self.copy(src, dst, recv, device, slot).start()

    def recv(self, dst, sem):
        self.copy(dst, dst, sem, self.at_x(1)).wait_recv()

    def sent(self, ref, slot):
        self.copy(ref, ref, self.rsem, self.at_x(1), slot).wait_send()

    def greet(self, peers):
        barrier = pltpu.get_barrier_semaphore()
        for peer in peers:
            pl.semaphore_signal(barrier, inc=1, device_id=peer, device_id_type=pl.DeviceIdType.MESH)
        return lambda: pl.semaphore_wait(barrier, len(peers))


def block(b):
    return pl.ds(pl.multiple_of(b * BLK, BLK), BLK)


def split_rows(ref, b):
    parts = [split(ref[pl.ds(2 * BLK * b + h, BLK, stride=2), :]) for h in (0, 1)]
    return tuple(jnp.concatenate(p, axis=1) for p in zip(*parts))


def gather(t, buf4, slot, sems, work):
    agaz, agax, agbx, agbz = sems
    x, z, own, other = t.x, t.z, t.x // 2, 1 - t.x // 2
    mod, at_x, at_z, send, recv = t.mod, t.at_x, t.at_z, t.send, t.recv

    def piece(xi, zi, lo=0, size=CA):
        return buf4.at[xi, zi, pl.ds(lo, size)]

    def pair(g, zi):
        return buf4.at[pl.ds(2 * g, 2), zi, pl.ds(CA, CB)]

    def side(zi, k):
        send(piece(x, zi), piece(x, zi), agax.at[0, k], at_x(1), slot)
        send(piece(x, zi), piece(x, zi), agax.at[1, k], at_x(-1), slot)

    def forward(zi, k):
        left, right = mod(x - 1, NX), mod(x + 1, NX)
        recv(piece(left, zi), agax.at[0, k])
        send(piece(left, zi, 0, CA // 2), piece(left, zi, 0, CA // 2), agax.at[2, k], at_x(1), slot)
        recv(piece(right, zi), agax.at[1, k])
        send(piece(right, zi, CA // 2, CA // 2), piece(right, zi, CA // 2, CA // 2), agax.at[3, k], at_x(-1), slot)

    def finish(zi, k):
        far = mod(x + 2, NX)
        recv(piece(far, zi, 0, CA // 2), agax.at[2, k])
        recv(piece(far, zi, CA // 2, CA // 2), agax.at[3, k])

    for d in (1, 2, 3):
        send(piece(x, z, CA, CB), piece(x, z, CA, CB), agbx.at[d], at_x(d), slot)
    send(piece(x, z), piece(x, z), agaz.at[0, 1], at_z(1), slot)
    send(piece(x, z), piece(x, z), agaz.at[1, 1], at_z(-1), slot)
    side(z, 0)
    for d in (1, 2, 3):
        recv(piece(mod(x - d, NX), z, CA, CB), agbx.at[d])
    for i, g in enumerate((own, other)):
        send(pair(g, z), pair(g, z), agbz.at[0, i, 1], at_z(1), slot)
        send(pair(g, z), pair(g, z), agbz.at[1, i, 1], at_z(-1), slot)

    def step(s, carry):
        zr, zl = mod(z - s, NZ), mod(z + s, NZ)
        recv(piece(x, zr), agaz.at[0, s])
        send(piece(x, zr), piece(x, zr), agaz.at[0, s + 1], at_z(1), slot)
        recv(piece(x, zl), agaz.at[1, s])

        @pl.when(s < 7)
        def _():
            send(piece(x, zl), piece(x, zl), agaz.at[1, s + 1], at_z(-1), slot)

        side(zr, s)
        side(zl, 8 + s)
        for i, g in enumerate((own, other)):
            recv(pair(g, zl), agbz.at[1, i, s])
            send(pair(g, zl), pair(g, zl), agbz.at[1, i, s + 1], at_z(-1), slot)
            recv(pair(g, zr), agbz.at[0, i, s])

            @pl.when(s < 7)
            def _():
                send(pair(g, zr), pair(g, zr), agbz.at[0, i, s + 1], at_z(1), slot)

        forward(mod(z - s + 1, NZ), s - 1)

        @pl.when(s > 1)
        def _():
            forward(mod(z + s - 1, NZ), 7 + s)

        work(s)
        return carry

    lax.fori_loop(1, 8, step, 0)
    far = mod(z + 8, NZ)
    recv(piece(x, far), agaz.at[0, 8])
    side(far, 8)
    forward(mod(z - 7, NZ), 7)
    forward(mod(z + 7, NZ), 15)
    for i, g in enumerate((own, other)):
        recv(pair(g, far), agbz.at[1, i, 8])
    forward(far, 8)

    def last(k, carry):
        finish(mod(jnp.where(k > 8, z + k - 8, z - k), NZ), k)
        return carry

    lax.fori_loop(0, 16, last, 0)
    t.sent(buf4.reshape(NX * NZ * CH, 128).at[pl.ds(0, 6552)], slot)


def panel_kernel(mom, grad, fac, panel, thi, tlo, momv, gradv, bhi, blo, gat, ppart, precv,
                 lsem, ssem, agaz, agax, agbx, agbz, psem):
    t = Links(ssem, agbx.at[0])
    r, c, mod, at_c, send, recv, sent = t.r, t.c, t.mod, t.at_c, t.send, t.recv, t.sent
    loads = (pltpu.make_async_copy(mom, momv, lsem.at[0]), pltpu.make_async_copy(grad, gradv, lsem.at[1]))
    for load in loads:
        load.start()
    greeted = t.greet([t.at_x(d) for d in (1, 2, 3)] + [at_c(d) for d in range(1, NC)] + [t.at_z(1), t.at_z(-1)])
    gat2 = gat.reshape(NX * NZ * CH, 128)

    gat2[pl.ds(CH * r, CH // 2, stride=2), :] = fac[:, :128]
    gat2[pl.ds(CH * r + 1, CH // 2, stride=2), :] = fac[:, 128:]
    greeted()

    def prepare(b):
        at = block(b)
        value = momv[:, at] + gradv[:, at].astype(F32)
        high, low = split(value)
        bhi[:, at], blo[:, at] = high, low
        high, low = split(value.T)
        thi[at, :], tlo[at, :] = high, low

    def prepare_step(s):
        @pl.when(s == 1)
        def _():
            for load in loads:
                load.wait()

        prepare(2 * s - 2)

        @pl.when(s < 7)
        def _():
            prepare(2 * s - 1)

    gather(t, gat, 0, (agaz, agax, agbx, agbz), prepare_step)

    def panel_step(b, total):
        at = block(b)
        return total + dot3((bhi[:, at], blo[:, at]), split_rows(gat2, b))

    total = lax.fori_loop(0, NBLK, panel_step, jnp.zeros((ROWS, RANK), F32))
    ppart[...] = total.reshape(NC, ROWS // NC, RANK)
    for d in range(1, NC):
        peer = mod(c + d, NC)
        send(ppart.at[peer], precv.at[d], psem.at[0, d], at_c(d), 1)
    mine = ppart[c]
    for d in range(1, NC):
        recv(precv.at[d], psem.at[0, d])
        mine = mine + precv[d]
    panel[c] = mine
    for d in range(1, NC):
        send(panel.at[c], panel.at[c], psem.at[1, d], at_c(d), 1)
    for d in range(1, NC):
        recv(panel.at[mod(c - d, NC)], psem.at[1, d])
    sent(gat2.at[pl.ds(0, 14 * 32)], 1)


def factor_kernel(panel, thi, tlo, rfh, rfl, basis, update, ownf,
                  part, red, xh, xf, za, zb, xb, gram, g0, g1, g2, g3, g4, aw, rfhv, rflv, sq, sqr,
                  ssem, agaz, agax, agbx, agbz, rsx, rsza, rszb, rsxb, gsem, qsem, osem, *, n_cols, scale):
    links = Links(ssem, agbx.at[0])
    r, c, x, z, mod = links.r, links.c, links.x, links.z, links.mod
    at_x, at_z, at_c, at_q = links.at_x, links.at_z, links.at_c, links.at_q
    send, recv, sent = links.send, links.recv, links.sent
    greeted = links.greet([at_x(d) for d in (1, 2, 3)] + [at_c(d) for d in range(1, NC)]
                      + [at_z(d) for d in (1, -1, 4, 8, 12)] + [at_q(d) for d in (1, 2, 3)])
    part2 = part.reshape(NX * NZ * CH, 128)
    red2 = red.reshape(NX * NZ * CH, 128)
    own, other = x // 2, 1 - x // 2

    left = panel[...]
    gram[...] = dot6(left.T, left)
    greeted()
    for d in (1, 2, 3):
        src = gram.at[pl.ds(pl.multiple_of(32 * c + 8 * mod(x + d, NX), 8), 8)]
        send(src, g0.at[d], gsem.at[0, d], at_x(d), 2)

    def gram_0():
        total = gram[pl.ds(pl.multiple_of(32 * c + 8 * x, 8), 8), :]
        for d in (1, 2, 3):
            recv(g0.at[d], gsem.at[0, d])
            total = total + g0[d]
        g1[0] = total
        for d in (1, 2, 3):
            send(g1.at[0], g1.at[d], gsem.at[1, d], at_q(d), 2)

    def gram_1():
        total = g1[0]
        for d in (1, 2, 3):
            recv(g1.at[d], gsem.at[1, d])
            total = total + g1[d]
        g2[0] = total
        for d in (1, 2, 3):
            send(g2.at[0], g2.at[d], gsem.at[2, d], at_z(4 * d), 2)

    def gram_2():
        total = g2[0]
        for d in (1, 2, 3):
            recv(g2.at[d], gsem.at[2, d])
            total = total + g2[d]
        g3[x] = total
        for d in (1, 2, 3):
            send(g3.at[x], g3.at[x], gsem.at[3, d], at_x(d), 2)

    def gram_3():
        for d in (1, 2, 3):
            recv(g3.at[mod(x - d, NX)], gsem.at[3, d])
        g4[c] = g3[...]
        for d in range(1, NC):
            send(g4.at[c], g4.at[c], gsem.at[4, d], at_c(d), 3)

    def gram_4():
        for d in range(1, NC):
            recv(g4.at[mod(c - d, NC)], gsem.at[4, d])
        aw[...] = g4[...].reshape(RANK, RANK)
        sent(gram.at[pl.ds(0, 96)], 2)
        sent(g4.at[pl.ds(0, NC - 1)], 3)

    lp = split(left)

    def term_step(b, carry):
        at = block(b)
        h = dot3((thi[at, :], tlo[at, :]), lp)
        part2[pl.ds(2 * BLK * b, BLK, stride=2), :] = h[:, :128]
        part2[pl.ds(2 * BLK * b + 1, BLK, stride=2), :] = h[:, 128:]
        return carry

    lax.fori_loop(0, NBLK, term_step, 0)

    xr, xl, xo = mod(x + 1, NX), mod(x - 1, NX), mod(x + 2, NX)
    half = CA // 2

    def send_half(zi, k):
        send(part.at[xo, zi, pl.ds(0, half)], xh.at[0, k], rsx.at[0, k], at_x(1), 4)
        send(part.at[xo, zi, pl.ds(half, half)], xh.at[1, k], rsx.at[1, k], at_x(-1), 4)

    def send_full(zi, k):
        recv(xh.at[0, k], rsx.at[0, k])
        part[xr, zi, :half, :] += xh[0, k]
        send(part.at[xr, zi, pl.ds(0, CA)], xf.at[0, k], rsx.at[2, k], at_x(1), 4)
        recv(xh.at[1, k], rsx.at[1, k])
        part[xl, zi, half:CA, :] += xh[1, k]
        send(part.at[xl, zi, pl.ds(0, CA)], xf.at[1, k], rsx.at[3, k], at_x(-1), 4)

    def take_full(zi, k):
        recv(xf.at[0, k], rsx.at[2, k])
        recv(xf.at[1, k], rsx.at[3, k])
        part[x, zi, :CA, :] += xf[0, k] + xf[1, k]

    def to_right(t):
        return mod(z + 8 - t, NZ)

    def to_left(t):
        return mod(z - 7 + t, NZ)

    for t in (0, 1):
        send_half(to_right(t), t)
        send_half(to_left(t), 8 + t)
    send_full(to_right(0), 0)
    send_full(to_left(0), 8)

    def reduce_step(t, carry):
        @pl.when(t < 6)
        def _():
            send_half(to_right(t + 2), t + 2)

        @pl.when(t < 6)
        def _():
            send_half(to_left(t + 2), 10 + t)

        @pl.when(t < 7)
        def _():
            send_full(to_right(t + 1), t + 1)

        @pl.when(t < 7)
        def _():
            send_full(to_left(t + 1), 9 + t)

        take_full(to_right(t), t)

        @pl.when(t > 0)
        def _():
            recv(za.at[0, t], rsza.at[0, t])
            part[x, to_right(t), :CA, :] += za[0, t]

        send(part.at[x, to_right(t), pl.ds(0, CA)], za.at[0, t + 1], rsza.at[0, t + 1], at_z(1), 4)

        @pl.when(t < 7)
        def _():
            take_full(to_left(t), 8 + t)

            @pl.when(t > 0)
            def _():
                recv(za.at[1, t], rsza.at[1, t])
                part[x, to_left(t), :CA, :] += za[1, t]

            send(part.at[x, to_left(t), pl.ds(0, CA)], za.at[1, t + 1], rsza.at[1, t + 1], at_z(-1), 4)

        bl, br = mod(z - 8 + t, NZ), mod(z + 7 - t, NZ)
        for i, g in enumerate((other, own)):
            rows = pl.ds(2 * g, 2)

            @pl.when(t > 0)
            def _():
                recv(zb.at[1, i, t], rszb.at[1, i, t])
                part[rows, bl, CA:, :] += zb[1, i, t]

            send(part.at[rows, bl, pl.ds(CA, CB)], zb.at[1, i, t + 1], rszb.at[1, i, t + 1], at_z(-1), 4)

            @pl.when(t < 7)
            def _():
                @pl.when(t > 0)
                def _():
                    recv(zb.at[0, i, t], rszb.at[0, i, t])
                    part[rows, br, CA:, :] += zb[0, i, t]

                send(part.at[rows, br, pl.ds(CA, CB)], zb.at[0, i, t + 1], rszb.at[0, i, t + 1], at_z(1), 4)

        for when, stage in enumerate((gram_0, gram_1, gram_2, gram_3, gram_4)):
            pl.when(t == when)(stage)
        return carry

    lax.fori_loop(0, 8, reduce_step, 0)
    for i, g in enumerate((other, own)):
        recv(zb.at[1, i, 8], rszb.at[1, i, 8])
        recv(zb.at[0, i, 7], rszb.at[0, i, 7])
        part[pl.ds(2 * g, 2), z, CA:, :] += zb[1, i, 8] + zb[0, i, 7]
    for d in (1, 2, 3):
        send(part.at[mod(x + d, NX), z, pl.ds(CA, CB)], xb.at[d], rsxb.at[d], at_x(d), 4)
    take_full(z, 15)
    recv(za.at[0, 8], rsza.at[0, 8])
    recv(za.at[1, 7], rsza.at[1, 7])
    red[x, z, :CA, :] = part[x, z, :CA, :] + (za[0, 8] + za[1, 7])
    total = part[x, z, CA:, :]
    for d in (1, 2, 3):
        recv(xb.at[d], rsxb.at[d])
        total = total + xb[d]
    red[x, z, CA:, :] = total
    sent(part2.at[pl.ds(0, 6552)], 4)

    sub = lax.broadcasted_iota(jnp.int32, (NB, 128), 0)
    lane = lax.broadcasted_iota(jnp.int32, (NB, 128), 1)
    sub_w = lax.broadcasted_iota(jnp.int32, (NB, RANK), 0)
    lane_w = lax.broadcasted_iota(jnp.int32, (NB, RANK), 1)
    i_all = lax.broadcasted_iota(jnp.int32, (RANK, RANK), 0)
    j_all = lax.broadcasted_iota(jnp.int32, (RANK, RANK), 1)

    def factor_block(k):
        first = pl.multiple_of(NB * k, NB)
        rows = aw[pl.ds(first, NB), :]
        near = jnp.where(k < 4, rows[:, :128], rows[:, 128:])
        near = pltpu.roll(near, lax.rem(128 - NB * lax.rem(k, 4), 128), 1)
        e = jnp.where(lane < NB, near, jnp.where(lane - NB == sub, 1.0, 0.0))
        for j in range(0, NB, 4):
            cols = [jnp.broadcast_to(e[:, j + i:j + i + 1], (NB, 128)) for i in range(4)]
            pivots = [e[j + i:j + i + 1, :] for i in range(4)]
            for i in range(4):
                at = slice(j + i, j + i + 1)
                ratio = jnp.where(sub > j + i, cols[i] * (1.0 / cols[i][at, :]), 0.0)
                for m in range(i + 1, 4):
                    cols[m] = cols[m] - ratio * cols[m][at, :]
                    pivots[m] = pivots[m] - ratio[j + m:j + m + 1, :] * pivots[i]
                e = e - ratio * pivots[i]
        diagonal = jnp.sum(jnp.where(lane == sub, e, 0.0), axis=1, keepdims=True)
        inverse = (e * (1.0 / jnp.sqrt(diagonal)))[:, NB:2 * NB]
        here = (lane_w >= first) & (lane_w < first + NB)
        rows = jnp.where(here, jnp.where(lane_w - first == sub_w, 1.0, 0.0), rows)
        rows = dot6(inverse, rows)
        below = jnp.where(lane_w >= first + NB, rows, 0.0)
        done = (i_all >= first + NB) & (j_all >= first) & (j_all < first + NB)
        aw[...] = jnp.where(done, 0.0, aw[...]) - dot6(below.T, rows)
        aw[pl.ds(first, NB), :] = rows

    gather(links, red, 5, (agaz, agax, agbx, agbz), lambda s: factor_block(s - 1))
    factor_block(7)

    inverse = jnp.where(i_all >= j_all, aw[...], 0.0)
    nt = ((1,), (1,))
    inv = split(inverse)

    def right_step(b, squares):
        rf = dot3(split_rows(red2, b), inv, nt)
        rfhv[block(b), :], rflv[block(b), :] = split(rf)
        return squares + jnp.sum((rf * rf).reshape(BLK // 8, 8, RANK), axis=0)

    squares = lax.fori_loop(0, NBLK, right_step, jnp.zeros((8, RANK), F32))
    stores = (pltpu.make_async_copy(rfhv, rfh, osem.at[0]), pltpu.make_async_copy(rflv, rfl, osem.at[1]))
    for store in stores:
        store.start()
    sq[...] = squares
    for d in range(1, NC):
        send(sq, sqr.at[d], qsem.at[d], at_c(d), 6)
    left_basis = dot6(left, inverse, nt)
    halves = [red2[pl.ds(CH * r + h, CH // 2, stride=2), :] for h in (0, 1)]
    own_rf = dot6(jnp.concatenate(halves, axis=1), inverse, nt)
    for d in range(1, NC):
        recv(sqr.at[d], qsem.at[d])
        squares = squares + sqr[d]
    rms = jnp.sqrt(jnp.sum(squares, axis=0, keepdims=True) * (1.0 / n_cols) + EPSILON)
    ownf[...] = own_rf / rms
    basis[...] = left_basis * -(1.0 - MOMENTUM_KEEP)
    update[...] = left_basis * (-scale / rms)
    sent(gram.at[pl.ds(0, 8 * (NC - 1))], 6)
    for store in stores:
        store.wait()


def output_kernel(mom, grad, rfh, rfl, basis, update, ownf, momo, wupd, faco):
    nt = ((1,), (1,))
    right = (rfh[...], rfl[...])
    momo[...] = mom[...] + grad[...].astype(F32) + dot3(split(basis[...]), right, nt)
    wupd[...] = dot3(split(update[...]), right, nt).astype(BF16)

    @pl.when(pl.program_id(0) == 0)
    def _():
        faco[...] = ownf[...]


def shards(momentum, gradient, factor):
    rows = momentum.shape[0] * lax.axis_size("row")
    n_cols = momentum.shape[1] * lax.axis_size("col")
    scale = STEP_SIZE * math.sqrt(rows / factor.shape[1])
    dma, vmem, hbm = pltpu.SemaphoreType.DMA, pltpu.VMEM, pl.BlockSpec(memory_space=pl.ANY)
    inside = pl.BlockSpec(memory_space=pltpu.VMEM)
    shape = jax.ShapeDtypeStruct
    flat = vmem((NX, NZ, CH, 128), F32)
    gather_sems = [dma((2, 9)), dma((4, 16)), dma((4,)), dma((2, 2, 9))]
    rows16 = vmem((NC, ROWS // NC, RANK), F32)
    panel, thi, tlo = pl.pallas_call(
        panel_kernel,
        out_shape=(shape((NC, ROWS // NC, RANK), F32), shape((COLS, ROWS), BF16), shape((COLS, ROWS), BF16)),
        in_specs=[hbm, hbm, inside],
        out_specs=(inside, inside, inside),
        scratch_shapes=[
            vmem((ROWS, COLS), F32), vmem((ROWS, COLS), BF16), vmem((ROWS, COLS), BF16), vmem((ROWS, COLS), BF16),
            flat, rows16, rows16, dma((2,)), dma((2,)), *gather_sems, dma((2, NC)),
        ],
        compiler_params=pltpu.CompilerParams(collective_id=0, has_side_effects=True, vmem_limit_bytes=40 * 2**20),
        name="left_panel",
    )(momentum, gradient, factor)
    small = vmem((4, 8, RANK), F32)
    rfh, rfl, basis, update, ownf = pl.pallas_call(
        functools.partial(factor_kernel, n_cols=n_cols, scale=scale),
        out_shape=(
            shape((COLS, RANK), BF16), shape((COLS, RANK), BF16),
            shape((ROWS, RANK), F32), shape((ROWS, RANK), F32), shape((CH // 2, RANK), F32)),
        in_specs=[inside, inside, inside],
        out_specs=(hbm, hbm, inside, inside, inside),
        scratch_shapes=[
            flat, flat, vmem((2, 16, CA // 2, 128), F32), vmem((2, 16, CA, 128), F32),
            vmem((2, 9, CA, 128), F32), vmem((2, 2, 9, 2, CB, 128), F32), vmem((4, CB, 128), F32),
            vmem((RANK, RANK), F32), small, small, small, small, vmem((NC, 4, 8, RANK), F32),
            vmem((RANK, RANK), F32), vmem((COLS, RANK), BF16), vmem((COLS, RANK), BF16),
            vmem((8, RANK), F32), vmem((NC, 8, RANK), F32),
            dma((7,)), *gather_sems, dma((4, 16)), dma((2, 9)), dma((2, 2, 9)), dma((4,)),
            dma((5, NC)), dma((NC,)), dma((2,)),
        ],
        compiler_params=pltpu.CompilerParams(collective_id=1, has_side_effects=True, vmem_limit_bytes=48 * 2**20),
        name="right_factor",
    )(panel.reshape(ROWS, RANK), thi, tlo)
    whole = pl.BlockSpec((ROWS, RANK), lambda b: (0, 0))
    across = pl.BlockSpec((ROWS, BLK), lambda b: (0, b))
    down = pl.BlockSpec((BLK, RANK), lambda b: (b, 0))
    chunk = pl.BlockSpec((CH // 2, RANK), lambda b: (0, 0))
    return pl.pallas_call(
        output_kernel,
        grid=(NBLK,),
        out_shape=(shape((ROWS, COLS), F32), shape((ROWS, COLS), BF16), shape((CH // 2, RANK), F32)),
        in_specs=[across, across, down, down, whole, whole, chunk],
        out_specs=(across, across, chunk),
        compiler_params=pltpu.CompilerParams(vmem_limit_bytes=24 * 2**20),
        name="outputs",
    )(momentum, gradient, rfh, rfl, basis, update, ownf)


def solution(mesh):
    placed = (P("row", "col"), P("row", "col"), P(("col", "row"), None))
    return jax.shard_map(shards, mesh=mesh, in_specs=placed, out_specs=placed, check_vma=False)
```

```python
import functools
import math

import jax
import jax.numpy as jnp
from jax import lax
from jax.experimental import pallas as pl
from jax.experimental.pallas import tpu as pltpu
from jax.sharding import PartitionSpec as P

HIGHEST = lax.Precision.HIGHEST
MOMENTUM_KEEP = 0.8
STEP_SIZE = 0.3
EPSILON = 1e-06
F32 = jnp.float32
BF16 = jnp.bfloat16

NX, NZ = 4, 16
NC = 8
CH = 104
CA = 64
CB = CH - CA
ROWS, COLS, RANK = 128, 3328, 256
BLK = 256
NBLK = COLS // BLK
NB = 32


def split(value):
    high = value.astype(BF16)
    return high, (value - high.astype(F32)).astype(BF16)


def dot(a, b, dims=((1,), (0,))):
    return lax.dot_general(a, b, (dims, ((), ())), preferred_element_type=F32)


def dot3(a, b, dims=((1,), (0,))):
    return dot(a[0], b[0], dims) + (dot(a[0], b[1], dims) + dot(a[1], b[0], dims))


def dot6(a, b, dims=((1,), (0,))):
    return lax.dot_general(a, b, (dims, ((), ())), precision=HIGHEST, preferred_element_type=F32)


class Links:
    def __init__(self, ssem, rsem):
        self.ssem, self.rsem = ssem, rsem
        self.r, self.c = lax.axis_index("row"), lax.axis_index("col")
        self.x, self.z = self.r // NZ, self.r % NZ

        x, z, c = self.x, self.z, self.c
        self.xs = {d: {"row": lax.rem(x + d, NX) * NZ + z, "col": c} for d in (1, 2, 3)}
        self.zs = {d: {"row": x * NZ + lax.rem(z + d, NZ), "col": c} for d in (1, 4, 8, 12, 15)}
        self.qs = {d: {"row": x * NZ + (z // 4) * 4 + lax.rem(z + d, 4), "col": c} for d in (1, 2, 3)}
        self.cs = {d: {"row": self.r, "col": lax.rem(c + d, NC)} for d in range(1, NC)}

    def copy(self, src, dst, recv, device, slot=0):
        return pltpu.make_async_remote_copy(
            src_ref=src, dst_ref=dst, send_sem=self.ssem.at[slot], recv_sem=recv,
            device_id=device, device_id_type=pl.DeviceIdType.MESH)

    def send(self, src, dst, recv, device, slot):
        self.copy(src, dst, recv, device, slot).start()

    def recv(self, dst, sem):
        self.copy(dst, dst, sem, self.xs[1]).wait_recv()

    def sent(self, ref, slot):
        self.copy(ref, ref, self.rsem, self.xs[1], slot).wait_send()

    def greet(self, peers):
        barrier = pltpu.get_barrier_semaphore()
        for peer in peers:
            pl.semaphore_signal(barrier, inc=1, device_id=peer, device_id_type=pl.DeviceIdType.MESH)
        return lambda: pl.semaphore_wait(barrier, len(peers))


def block(b):
    return pl.ds(pl.multiple_of(b * BLK, BLK), BLK)


def split_rows(ref, b):
    parts = [split(ref[pl.ds(2 * BLK * b + h, BLK, stride=2), :]) for h in (0, 1)]
    return tuple(jnp.concatenate(p, axis=1) for p in zip(*parts))


def gather(t, buf, natural, sems, work):
    agaz, agax, agbx, agbz = sems
    xs, send, recv = t.xs, t.send, t.recv
    right, left = t.zs[1], t.zs[15]
    half = CA // 2

    def one(k):
        return buf.at[0, k, pl.ds(0, CA)]

    def two(i, k, n, lo=0, size=CA):
        return buf.at[i, pl.ds(k, n), pl.ds(lo, size)]

    def group(g, k):
        return buf.at[pl.ds(2 * g, 2), k, pl.ds(CA, CB)]

    def side(k, n, s):
        send(two(0, k, n), two(1, k, n), agax.at[0, s], xs[1], 0)
        send(two(0, k, n), two(3, k, n), agax.at[1, s], xs[3], 0)

    def forward(k, n, s):
        recv(two(1, k, n), agax.at[0, s])
        send(two(1, k, n, 0, half), two(2, k, n, 0, half), agax.at[2, s], xs[1], 0)
        recv(two(3, k, n), agax.at[1, s])
        send(two(3, k, n, half, half), two(2, k, n, half, half), agax.at[3, s], xs[3], 0)

    def finish(k, n, s):
        recv(two(2, k, n, 0, half), agax.at[2, s])
        recv(two(2, k, n, half, half), agax.at[3, s])

    for d in (1, 2, 3):
        send(buf.at[0, 0, pl.ds(CA, CB)], buf.at[d, 0, pl.ds(CA, CB)], agbx.at[d], xs[d], 0)
    send(one(0), one(1), agaz.at[0, 1], right, 0)
    send(one(0), one(2), agaz.at[1, 1], left, 0)
    side(0, 1, 0)
    for d in (1, 2, 3):
        recv(buf.at[d, 0, pl.ds(CA, CB)], agbx.at[d])
    for g in (0, 1):
        send(group(g, 0), group(g, 1), agbz.at[0, g, 1], right, 0)
        send(group(g, 0), group(g, 2), agbz.at[1, g, 1], left, 0)
    forward(0, 1, 0)

    def step(s, carry):
        kr, kl = 2 * s - 1, 2 * s
        recv(one(kr), agaz.at[0, s])
        send(one(kr), one(kr + 2), agaz.at[0, s + 1], right, 0)
        recv(one(kl), agaz.at[1, s])

        @pl.when(s < 7)
        def _():
            send(one(kl), one(kl + 2), agaz.at[1, s + 1], left, 0)

        side(kr, 2, s)
        for g in (0, 1):
            recv(group(g, kl), agbz.at[1, g, s])
            send(group(g, kl), group(g, jnp.minimum(kl + 2, 15)), agbz.at[1, g, s + 1], left, 0)
            recv(group(g, kr), agbz.at[0, g, s])

            @pl.when(s < 7)
            def _():
                send(group(g, kr), group(g, kr + 2), agbz.at[0, g, s + 1], right, 0)

        @pl.when(s > 1)
        def _():
            forward(kr - 2, 2, s - 1)

        work(s)
        return carry

    lax.fori_loop(1, 8, step, 0)
    recv(one(15), agaz.at[0, 8])
    side(15, 1, 8)
    forward(13, 2, 7)
    for g in (0, 1):
        recv(group(g, 15), agbz.at[1, g, 8])
    forward(15, 1, 8)
    finish(0, 1, 0)

    def last(s, carry):
        finish(2 * s - 1, 2, s)
        return carry

    lax.fori_loop(1, 8, last, 0)
    finish(15, 1, 8)
    t.sent(buf.reshape(NX * NZ * CH, 128).at[pl.ds(0, 6552)], 0)

    def place(n, carry):
        s = lax.rem(t.z - n + 2 * NZ, NZ)
        k = jnp.where(s == 0, 0, jnp.where(s > 8, 2 * (NZ - s), 2 * s - 1))
        for i in range(NX):
            row = lax.rem(t.x - i + NX, NX) * NZ + n
            natural[pl.ds(pl.multiple_of(CH * row, 8), CH), :] = buf[i, k]
        return carry

    lax.fori_loop(0, NZ, place, 0)


def panel_kernel(mom, grad, fac, panel, thi, tlo, momv, gradv, bhi, blo, gat, gat2, ppart, precv,
                 lsem, ssem, agaz, agax, agbx, agbz, psem):
    t = Links(ssem, agbx.at[0])
    c, cs, send, recv, sent = t.c, t.cs, t.send, t.recv, t.sent
    loads = (pltpu.make_async_copy(mom, momv, lsem.at[0]), pltpu.make_async_copy(grad, gradv, lsem.at[1]))
    for load in loads:
        load.start()
    greeted = t.greet([*t.xs.values(), *cs.values(), t.zs[1], t.zs[15]])

    gat.at[0, 0][pl.ds(0, CH // 2, stride=2), :] = fac[:, :128]
    gat.at[0, 0][pl.ds(1, CH // 2, stride=2), :] = fac[:, 128:]
    greeted()

    def prepare(b):
        at = block(b)
        value = momv[:, at] + gradv[:, at].astype(F32)
        high, low = split(value)
        bhi[:, at], blo[:, at] = high, low
        high, low = split(value.T)
        thi[at, :], tlo[at, :] = high, low

    def prepare_step(s):
        @pl.when(s == 1)
        def _():
            for load in loads:
                load.wait()

        prepare(2 * s - 2)

        @pl.when(s < 7)
        def _():
            prepare(2 * s - 1)

    gather(t, gat, gat2, (agaz, agax, agbx, agbz), prepare_step)

    def panel_step(b, total):
        at = block(b)
        return total + dot3((bhi[:, at], blo[:, at]), split_rows(gat2, b))

    total = lax.fori_loop(0, NBLK, panel_step, jnp.zeros((ROWS, RANK), F32))
    ppart[...] = total.reshape(NC, ROWS // NC, RANK)
    for d in range(1, NC):
        send(ppart.at[cs[d]["col"]], precv.at[d], psem.at[0, d], cs[d], 1)
    mine = ppart[c]
    for d in range(1, NC):
        recv(precv.at[d], psem.at[0, d])
        mine = mine + precv[d]
    panel[c] = mine
    for d in range(1, NC):
        send(panel.at[c], panel.at[c], psem.at[1, d], cs[d], 1)
    for d in range(1, NC):
        recv(panel.at[lax.rem(c - d + NC, NC)], psem.at[1, d])
    sent(gat2.at[pl.ds(0, 14 * 32)], 1)


def factor_kernel(panel, thi, tlo, rfh, rfl, basis, update, ownf,
                  term, part, red, red2, xh, xf, za, zb, xb, gram, g0, g1, g2, g3, g4, aw, rfhv, rflv, sq, sqr,
                  ssem, agaz, agax, agbx, agbz, rsx, rsza, rszb, rsxb, gsem, qsem, osem, *, n_cols, scale):
    t = Links(ssem, agbx.at[0])
    r, c, x, z = t.r, t.c, t.x, t.z
    xs, zs, qs, cs, send, recv, sent = t.xs, t.zs, t.qs, t.cs, t.send, t.recv, t.sent
    greeted = t.greet([*xs.values(), *zs.values(), *qs.values(), *cs.values()])

    left = panel[...]
    gram[...] = dot6(left.T, left)
    greeted()

    def gram_rows(xi):
        return pl.ds(pl.multiple_of(32 * c + 8 * xi, 8), 8)

    for d in (1, 2, 3):
        send(gram.at[gram_rows(lax.rem(x + d, NX))], g0.at[d], gsem.at[0, d], xs[d], 2)

    def gram_0():
        total = gram[gram_rows(x), :]
        for d in (1, 2, 3):
            recv(g0.at[d], gsem.at[0, d])
            total = total + g0[d]
        g1[0] = total
        for d in (1, 2, 3):
            send(g1.at[0], g1.at[d], gsem.at[1, d], qs[d], 2)

    def gram_1():
        total = g1[0]
        for d in (1, 2, 3):
            recv(g1.at[d], gsem.at[1, d])
            total = total + g1[d]
        g2[0] = total
        for d in (1, 2, 3):
            send(g2.at[0], g2.at[d], gsem.at[2, d], zs[4 * d], 2)

    def gram_2():
        total = g2[0]
        for d in (1, 2, 3):
            recv(g2.at[d], gsem.at[2, d])
            total = total + g2[d]
        g3[x] = total
        for d in (1, 2, 3):
            send(g3.at[x], g3.at[x], gsem.at[3, d], xs[d], 2)

    def gram_3():
        for d in (1, 2, 3):
            recv(g3.at[lax.rem(x - d + NX, NX)], gsem.at[3, d])
        g4[c] = g3[...]
        for d in range(1, NC):
            send(g4.at[c], g4.at[c], gsem.at[4, d], cs[d], 3)

    def gram_4():
        for d in range(1, NC):
            recv(g4.at[lax.rem(c - d + NC, NC)], gsem.at[4, d])
        aw[...] = g4[...].reshape(RANK, RANK)
        sent(gram.at[pl.ds(0, 96)], 2)
        sent(g4.at[pl.ds(0, NC - 1)], 3)

    sub = lax.broadcasted_iota(jnp.int32, (NB, 128), 0)
    lane = lax.broadcasted_iota(jnp.int32, (NB, 128), 1)
    sub_w = lax.broadcasted_iota(jnp.int32, (NB, RANK), 0)
    lane_w = lax.broadcasted_iota(jnp.int32, (NB, RANK), 1)
    i_all = lax.broadcasted_iota(jnp.int32, (RANK, RANK), 0)
    j_all = lax.broadcasted_iota(jnp.int32, (RANK, RANK), 1)

    def factor_block(k):
        first = pl.multiple_of(NB * k, NB)
        rows = aw[pl.ds(first, NB), :]
        near = jnp.where(k < 4, rows[:, :128], rows[:, 128:])
        near = pltpu.roll(near, lax.rem(128 - NB * lax.rem(k, 4), 128), 1)
        e = jnp.where(lane < NB, near, jnp.where(lane - NB == sub, 1.0, 0.0))
        for j in range(0, NB, 4):
            cols = [jnp.broadcast_to(e[:, j + i:j + i + 1], (NB, 128)) for i in range(4)]
            pivots = [e[j + i:j + i + 1, :] for i in range(4)]
            for i in range(4):
                at = slice(j + i, j + i + 1)
                ratio = jnp.where(sub > j + i, cols[i] * (1.0 / cols[i][at, :]), 0.0)
                for m in range(i + 1, 4):
                    cols[m] = cols[m] - ratio * cols[m][at, :]
                    pivots[m] = pivots[m] - ratio[j + m:j + m + 1, :] * pivots[i]
                e = e - ratio * pivots[i]
        diagonal = jnp.sum(jnp.where(lane == sub, e, 0.0), axis=1, keepdims=True)
        inverse = (e * (1.0 / jnp.sqrt(diagonal)))[:, NB:2 * NB]
        here = (lane_w >= first) & (lane_w < first + NB)
        rows = jnp.where(here, jnp.where(lane_w - first == sub_w, 1.0, 0.0), rows)
        rows = dot6(inverse, rows)
        below = jnp.where(lane_w >= first + NB, rows, 0.0)
        done = (i_all >= first + NB) & (j_all >= first) & (j_all < first + NB)
        aw[...] = jnp.where(done, 0.0, aw[...]) - dot6(below.T, rows)
        aw[pl.ds(first, NB), :] = rows

    lp = split(left)

    def term_step(b, carry):
        h = dot3((thi[block(b), :], tlo[block(b), :]), lp)
        term[pl.ds(2 * BLK * b, BLK, stride=2), :] = h[:, :128]
        term[pl.ds(2 * BLK * b + 1, BLK, stride=2), :] = h[:, 128:]
        pl.when(b == 6)(gram_0)
        return carry

    lax.fori_loop(0, NBLK, term_step, 0)
    gram_1()

    def place(k, carry):
        n = lax.rem(jnp.where(lax.rem(k, 2) == 0, z + 8 - k // 2, jnp.where(k == 15, z, z + 9 + k // 2)), NZ)
        for i in range(NX):
            row = lax.rem(x + i, NX) * NZ + n
            part[i, k] = term[pl.ds(pl.multiple_of(CH * row, 8), CH), :]
        return carry

    lax.fori_loop(0, NZ, place, 0)

    half = CA // 2

    def pair(i, s, lo=0, size=CA):
        return part.at[i, pl.ds(2 * s, 2), pl.ds(lo, size)]

    def send_half(s):
        send(pair(2, s, 0, half), xh.at[0, s], rsx.at[0, s], xs[1], 4)
        send(pair(2, s, half, half), xh.at[1, s], rsx.at[1, s], xs[3], 4)

    def send_full(s):
        two = pl.ds(2 * s, 2)
        recv(xh.at[0, s], rsx.at[0, s])
        part[1, two, :half, :] += xh[0, s]
        send(pair(1, s), xf.at[0, s], rsx.at[2, s], xs[1], 4)
        recv(xh.at[1, s], rsx.at[1, s])
        part[3, two, half:CA, :] += xh[1, s]
        send(pair(3, s), xf.at[1, s], rsx.at[3, s], xs[3], 4)

    def take_full(s):
        two = pl.ds(2 * s, 2)
        recv(xf.at[0, s], rsx.at[2, s])
        recv(xf.at[1, s], rsx.at[3, s])
        part[0, two, :CA, :] += xf[0, s] + xf[1, s]

    send_half(0)
    send_half(1)
    send_full(0)

    def reduce_step(s, carry):
        @pl.when(s < 6)
        def _():
            send_half(s + 2)

        for i, g in enumerate((1, 0)):
            rows = pl.ds(2 * g, 2)
            kl, kr = jnp.maximum(2 * s - 1, 0), 2 * s + 2

            @pl.when(s > 0)
            def _():
                recv(zb.at[1, i, s], rszb.at[1, i, s])
                part[rows, kl, CA:, :] += zb[1, i, s]

            send(part.at[rows, kl, pl.ds(CA, CB)], zb.at[1, i, s + 1], rszb.at[1, i, s + 1], zs[15], 4)

            @pl.when(s < 7)
            def _():
                @pl.when(s > 0)
                def _():
                    recv(zb.at[0, i, s], rszb.at[0, i, s])
                    part[rows, kr, CA:, :] += zb[0, i, s]

                send(part.at[rows, kr, pl.ds(CA, CB)], zb.at[0, i, s + 1], rszb.at[0, i, s + 1], zs[1], 4)

        @pl.when(s < 7)
        def _():
            send_full(s + 1)

        take_full(s)

        @pl.when(s > 0)
        def _():
            recv(za.at[0, s], rsza.at[0, s])
            part[0, 2 * s, :CA, :] += za[0, s]

        send(part.at[0, 2 * s, pl.ds(0, CA)], za.at[0, s + 1], rsza.at[0, s + 1], zs[1], 4)

        @pl.when(s < 7)
        def _():
            @pl.when(s > 0)
            def _():
                recv(za.at[1, s], rsza.at[1, s])
                part[0, 2 * s + 1, :CA, :] += za[1, s]

            send(part.at[0, 2 * s + 1, pl.ds(0, CA)], za.at[1, s + 1], rsza.at[1, s + 1], zs[15], 4)

        for when, stage in enumerate((gram_2, gram_3, gram_4)):
            pl.when(s == when)(stage)

        @pl.when(s > 2)
        def _():
            factor_block(s - 3)

        return carry

    lax.fori_loop(0, 8, reduce_step, 0)
    for i, g in enumerate((1, 0)):
        recv(zb.at[1, i, 8], rszb.at[1, i, 8])
        recv(zb.at[0, i, 7], rszb.at[0, i, 7])
        part[2 * g:2 * g + 2, 15, CA:, :] += zb[1, i, 8] + zb[0, i, 7]
    for d in (1, 2, 3):
        send(part.at[d, 15, pl.ds(CA, CB)], xb.at[d], rsxb.at[d], xs[d], 4)
    recv(za.at[0, 8], rsza.at[0, 8])
    recv(za.at[1, 7], rsza.at[1, 7])
    red[0, 0, :CA, :] = part[0, 15, :CA, :] + (za[0, 8] + za[1, 7])
    total = part[0, 15, CA:, :]
    for d in (1, 2, 3):
        recv(xb.at[d], rsxb.at[d])
        total = total + xb[d]
    red[0, 0, CA:, :] = total
    sent(term.at[pl.ds(0, 6552)], 4)

    def factor_rest(s):
        @pl.when(s < 4)
        def _():
            factor_block(s + 4)

    gather(t, red, red2, (agaz, agax, agbx, agbz), factor_rest)

    inverse = jnp.where(i_all >= j_all, aw[...], 0.0)
    nt = ((1,), (1,))
    inv = split(inverse)

    def right_step(b, squares):
        rf = dot3(split_rows(red2, b), inv, nt)
        rfhv[block(b), :], rflv[block(b), :] = split(rf)
        return squares + jnp.sum((rf * rf).reshape(BLK // 8, 8, RANK), axis=0)

    squares = lax.fori_loop(0, NBLK, right_step, jnp.zeros((8, RANK), F32))
    stores = (pltpu.make_async_copy(rfhv, rfh, osem.at[0]), pltpu.make_async_copy(rflv, rfl, osem.at[1]))
    for store in stores:
        store.start()
    sq[...] = squares
    for d in range(1, NC):
        send(sq, sqr.at[d], qsem.at[d], cs[d], 6)
    left_basis = dot6(left, inverse, nt)
    halves = [red.at[0, 0][pl.ds(h, CH // 2, stride=2), :] for h in (0, 1)]
    own_rf = dot6(jnp.concatenate(halves, axis=1), inverse, nt)
    for d in range(1, NC):
        recv(sqr.at[d], qsem.at[d])
        squares = squares + sqr[d]
    rms = jnp.sqrt(jnp.sum(squares, axis=0, keepdims=True) * (1.0 / n_cols) + EPSILON)
    ownf[...] = own_rf / rms
    basis[...] = left_basis * -(1.0 - MOMENTUM_KEEP)
    update[...] = left_basis * (-scale / rms)
    sent(gram.at[pl.ds(0, 8 * (NC - 1))], 6)
    for store in stores:
        store.wait()


def output_kernel(mom, grad, rfh, rfl, basis, update, ownf, momo, wupd, faco):
    nt = ((1,), (1,))
    high, low = split(update[...])
    rows = jnp.concatenate([basis[...].astype(BF16), high, low], axis=0)
    product = dot(rows, rfh[...], nt)
    momo[...] = mom[...] + grad[...].astype(F32) + product[:ROWS]
    wupd[...] = (product[ROWS:2 * ROWS] + (product[2 * ROWS:] + dot(high, rfl[...], nt))).astype(BF16)

    @pl.when(pl.program_id(0) == 0)
    def _():
        faco[...] = ownf[...]


def shards(momentum, gradient, factor):
    rows = momentum.shape[0] * lax.axis_size("row")
    n_cols = momentum.shape[1] * lax.axis_size("col")
    scale = STEP_SIZE * math.sqrt(rows / factor.shape[1])
    dma, vmem, hbm = pltpu.SemaphoreType.DMA, pltpu.VMEM, pl.BlockSpec(memory_space=pl.ANY)
    inside = pl.BlockSpec(memory_space=pltpu.VMEM)
    shape = jax.ShapeDtypeStruct
    flat, natural = vmem((NX, NZ, CH, 128), F32), vmem((NX * NZ * CH, 128), F32)
    gather_sems = [dma((2, 9)), dma((4, 9)), dma((4,)), dma((2, 2, 9))]
    rows16 = vmem((NC, ROWS // NC, RANK), F32)
    panel, thi, tlo = pl.pallas_call(
        panel_kernel,
        out_shape=(shape((NC, ROWS // NC, RANK), F32), shape((COLS, ROWS), BF16), shape((COLS, ROWS), BF16)),
        in_specs=[hbm, hbm, inside],
        out_specs=(inside, inside, inside),
        scratch_shapes=[
            vmem((ROWS, COLS), F32), vmem((ROWS, COLS), BF16), vmem((ROWS, COLS), BF16), vmem((ROWS, COLS), BF16),
            flat, natural, rows16, rows16, dma((2,)), dma((2,)), *gather_sems, dma((2, NC)),
        ],
        compiler_params=pltpu.CompilerParams(collective_id=0, has_side_effects=True, vmem_limit_bytes=60 * 2**20),
        name="left_panel",
    )(momentum, gradient, factor)
    small = vmem((4, 8, RANK), F32)
    rfh, rfl, basis, update, ownf = pl.pallas_call(
        functools.partial(factor_kernel, n_cols=n_cols, scale=scale),
        out_shape=(
            shape((COLS, RANK), BF16), shape((COLS, RANK), BF16),
            shape((ROWS, RANK), F32), shape((ROWS, RANK), F32), shape((CH // 2, RANK), F32)),
        in_specs=[inside, inside, inside],
        out_specs=(hbm, hbm, inside, inside, inside),
        scratch_shapes=[
            natural, flat, flat, natural, vmem((2, 8, 2, CA // 2, 128), F32), vmem((2, 8, 2, CA, 128), F32),
            vmem((2, 9, CA, 128), F32), vmem((2, 2, 9, 2, CB, 128), F32), vmem((4, CB, 128), F32),
            vmem((RANK, RANK), F32), small, small, small, small, vmem((NC, 4, 8, RANK), F32),
            vmem((RANK, RANK), F32), vmem((COLS, RANK), BF16), vmem((COLS, RANK), BF16),
            vmem((8, RANK), F32), vmem((NC, 8, RANK), F32),
            dma((7,)), *gather_sems, dma((4, 8)), dma((2, 9)), dma((2, 2, 9)), dma((4,)),
            dma((5, NC)), dma((NC,)), dma((2,)),
        ],
        compiler_params=pltpu.CompilerParams(collective_id=1, has_side_effects=True, vmem_limit_bytes=60 * 2**20),
        name="right_factor",
    )(panel.reshape(ROWS, RANK), thi, tlo)
    whole = pl.BlockSpec((ROWS, RANK), lambda b: (0, 0))
    across = pl.BlockSpec((ROWS, BLK), lambda b: (0, b))
    down = pl.BlockSpec((BLK, RANK), lambda b: (b, 0))
    chunk = pl.BlockSpec((CH // 2, RANK), lambda b: (0, 0))
    return pl.pallas_call(
        output_kernel,
        grid=(NBLK,),
        out_shape=(shape((ROWS, COLS), F32), shape((ROWS, COLS), BF16), shape((CH // 2, RANK), F32)),
        in_specs=[across, across, down, down, whole, whole, chunk],
        out_specs=(across, across, chunk),
        compiler_params=pltpu.CompilerParams(vmem_limit_bytes=60 * 2**20),
        name="outputs",
    )(momentum, gradient, rfh, rfl, basis, update, ownf)


def solution(mesh):
    placed = (P("row", "col"), P("row", "col"), P(("col", "row"), None))
    return jax.shard_map(shards, mesh=mesh, in_specs=placed, out_specs=placed, check_vma=False)
```

```python
import functools
import math

import jax
import jax.numpy as jnp
from jax import lax
from jax.experimental import pallas as pl
from jax.experimental.pallas import tpu as pltpu
from jax.sharding import PartitionSpec as P

HIGHEST = lax.Precision.HIGHEST
MOMENTUM_KEEP = 0.8
STEP_SIZE = 0.3
EPSILON = 1e-06
F32 = jnp.float32
BF16 = jnp.bfloat16

NX, NZ = 4, 16
NC = 8
CH = 104
CA = 64
CB = CH - CA
ROWS, COLS, RANK = 128, 3328, 256
BLK = 256
NBLK = COLS // BLK
HALF = COLS // 2
NB = 32


def split(value):
    high = value.astype(BF16)
    return high, (value - high.astype(F32)).astype(BF16)


def dot(a, b, dims=((1,), (0,))):
    return lax.dot_general(a, b, (dims, ((), ())), preferred_element_type=F32)


def dot3(a, b, dims=((1,), (0,))):
    return dot(a[0], b[0], dims) + (dot(a[0], b[1], dims) + dot(a[1], b[0], dims))


def dot6(a, b, dims=((1,), (0,))):
    return lax.dot_general(a, b, (dims, ((), ())), precision=HIGHEST, preferred_element_type=F32)


class Links:
    def __init__(self, ssem, rsem):
        self.ssem, self.rsem = ssem, rsem
        self.r, self.c = lax.axis_index("row"), lax.axis_index("col")
        self.x, self.z = self.r // NZ, self.r % NZ

        x, z, c = self.x, self.z, self.c
        self.xs = {d: {"row": lax.rem(x + d, NX) * NZ + z, "col": c} for d in (1, 2, 3)}
        self.zs = {d: {"row": x * NZ + lax.rem(z + d, NZ), "col": c} for d in (1, 4, 5, 8, 11, 12, 15)}
        self.qs = {d: {"row": x * NZ + (z // 4) * 4 + lax.rem(z + d, 4), "col": c} for d in (1, 2, 3)}
        self.cs = {d: {"row": self.r, "col": lax.rem(c + d, NC)} for d in range(1, NC)}

    def copy(self, src, dst, recv, device, slot=0):
        return pltpu.make_async_remote_copy(
            src_ref=src, dst_ref=dst, send_sem=self.ssem.at[slot], recv_sem=recv,
            device_id=device, device_id_type=pl.DeviceIdType.MESH)

    def send(self, src, dst, recv, device, slot):
        self.copy(src, dst, recv, device, slot).start()

    def recv(self, dst, sem):
        self.copy(dst, dst, sem, self.xs[1]).wait_recv()

    def sent(self, ref, slot):
        self.copy(ref, ref, self.rsem, self.xs[1], slot).wait_send()

    def greet(self, peers):
        barrier = pltpu.get_barrier_semaphore()
        peers = list(peers)
        for peer in peers:
            pl.semaphore_signal(barrier, inc=1, device_id=peer, device_id_type=pl.DeviceIdType.MESH)
        return lambda: pl.semaphore_wait(barrier, len(peers))


def block(b):
    return pl.ds(pl.multiple_of(b * BLK, BLK), BLK)


def split_rows(ref, b):
    parts = [split(ref[pl.ds(2 * BLK * b + h, BLK, stride=2), :]) for h in (0, 1)]
    return tuple(jnp.concatenate(p, axis=1) for p in zip(*parts))


def gather(t, buf, natural, sems, work):
    agaz, agax, agbx, agbz = sems
    xs, send, recv = t.xs, t.send, t.recv
    right, left = t.zs[1], t.zs[15]
    half = CA // 2

    def one(k):
        return buf.at[0, k, pl.ds(0, CA)]

    def two(i, k, n, lo=0, size=CA):
        return buf.at[i, pl.ds(k, n), pl.ds(lo, size)]

    def group(g, k):
        return buf.at[pl.ds(2 * g, 2), k, pl.ds(CA, CB)]

    def side(k, n, s):
        send(two(0, k, n), two(1, k, n), agax.at[0, s], xs[1], 0)
        send(two(0, k, n), two(3, k, n), agax.at[1, s], xs[3], 0)

    def forward(k, n, s):
        recv(two(1, k, n), agax.at[0, s])
        send(two(1, k, n, 0, half), two(2, k, n, 0, half), agax.at[2, s], xs[1], 0)
        recv(two(3, k, n), agax.at[1, s])
        send(two(3, k, n, half, half), two(2, k, n, half, half), agax.at[3, s], xs[3], 0)

    def finish(k, n, s):
        recv(two(2, k, n, 0, half), agax.at[2, s])
        recv(two(2, k, n, half, half), agax.at[3, s])

    for d in (1, 2, 3):
        send(buf.at[0, 0, pl.ds(CA, CB)], buf.at[d, 0, pl.ds(CA, CB)], agbx.at[d], xs[d], 0)
    send(one(0), one(1), agaz.at[0, 1], right, 0)
    send(one(0), one(2), agaz.at[1, 1], left, 0)
    side(0, 1, 0)
    for d in (1, 2, 3):
        recv(buf.at[d, 0, pl.ds(CA, CB)], agbx.at[d])
    for g in (0, 1):
        send(group(g, 0), group(g, 1), agbz.at[0, g, 1], right, 0)
        send(group(g, 0), group(g, 2), agbz.at[1, g, 1], left, 0)
    forward(0, 1, 0)

    def step(s, carry):
        kr, kl = 2 * s - 1, 2 * s
        recv(one(kr), agaz.at[0, s])
        send(one(kr), one(kr + 2), agaz.at[0, s + 1], right, 0)
        recv(one(kl), agaz.at[1, s])

        @pl.when(s < 7)
        def _():
            send(one(kl), one(kl + 2), agaz.at[1, s + 1], left, 0)

        side(kr, 2, s)
        for g in (0, 1):
            recv(group(g, kl), agbz.at[1, g, s])
            send(group(g, kl), group(g, jnp.minimum(kl + 2, 15)), agbz.at[1, g, s + 1], left, 0)
            recv(group(g, kr), agbz.at[0, g, s])

            @pl.when(s < 7)
            def _():
                send(group(g, kr), group(g, kr + 2), agbz.at[0, g, s + 1], right, 0)

        @pl.when(s > 1)
        def _():
            forward(kr - 2, 2, s - 1)

        work(s)
        return carry

    lax.fori_loop(1, 8, step, 0)
    recv(one(15), agaz.at[0, 8])
    side(15, 1, 8)
    forward(13, 2, 7)
    for g in (0, 1):
        recv(group(g, 15), agbz.at[1, g, 8])
    forward(15, 1, 8)
    finish(0, 1, 0)

    def last(s, carry):
        finish(2 * s - 1, 2, s)
        return carry

    lax.fori_loop(1, 8, last, 0)
    finish(15, 1, 8)
    t.sent(buf.reshape(NX * NZ * CH, 128).at[pl.ds(0, 6552)], 0)

    def place(n, carry):
        s = lax.rem(t.z - n + 2 * NZ, NZ)
        k = jnp.where(s == 0, 0, jnp.where(s > 8, 2 * (NZ - s), 2 * s - 1))
        for i in range(NX):
            row = lax.rem(t.x - i + NX, NX) * NZ + n
            natural[pl.ds(pl.multiple_of(CH * row, 8), CH), :] = buf[i, k]
        return carry

    lax.fori_loop(0, NZ, place, 0)


def gather_kernel(mom, grad, fac, gat2, bhi, blo, thi, tlo, momv, gradv, gat, lsem, ssem, *sems):
    t = Links(ssem, sems[0].at[0, 0])
    loads = (pltpu.make_async_copy(mom, momv, lsem.at[0]), pltpu.make_async_copy(grad, gradv, lsem.at[1]))
    for load in loads:
        load.start()
    greeted = t.greet([*t.xs.values(), t.zs[1], t.zs[15]])

    gat.at[0, 0][pl.ds(0, CH // 2, stride=2), :] = fac[:, :128]
    gat.at[0, 0][pl.ds(1, CH // 2, stride=2), :] = fac[:, 128:]
    greeted()

    def prepare(b):
        at = block(b)
        value = momv[:, at] + gradv[:, at].astype(F32)
        high, low = split(value)
        bhi[:, at], blo[:, at] = high, low
        high, low = split(value.T)
        thi[at, :], tlo[at, :] = high, low

    def prepare_step(s):
        @pl.when(s == 1)
        def _():
            for load in loads:
                load.wait()

        prepare(2 * s - 2)

        @pl.when(s < 7)
        def _():
            prepare(2 * s - 1)

    gather(t, gat, gat2, sems, prepare_step)


def panel_kernel(gat2, bhi, blo, panel, ppart, precv, ssem, psem):
    t = Links(ssem, psem.at[0, 0])
    c, cs, send, recv, sent = t.c, t.cs, t.send, t.recv, t.sent
    greeted = t.greet(cs.values())

    def panel_step(b, total):
        at = block(b)
        return total + dot3((bhi[:, at], blo[:, at]), split_rows(gat2, b))

    total = lax.fori_loop(0, NBLK, panel_step, jnp.zeros((ROWS, RANK), F32))
    ppart[...] = total.reshape(NC, ROWS // NC, RANK)
    greeted()
    for d in range(1, NC):
        send(ppart.at[cs[d]["col"]], precv.at[d], psem.at[0, d], cs[d], 0)
    mine = ppart[c]
    for d in range(1, NC):
        recv(precv.at[d], psem.at[0, d])
        mine = mine + precv[d]
    panel[c] = mine
    for d in range(1, NC):
        send(panel.at[c], panel.at[c], psem.at[1, d], cs[d], 0)
    for d in range(1, NC):
        recv(panel.at[lax.rem(c - d + NC, NC)], psem.at[1, d])
    sent(gat2.at[pl.ds(0, 14 * 32)], 0)


def factor_kernel(panel, thi, tlo, red2, lower, own,
                  term, part, red, xh, xf, za, zb, xb, gram, g0, g1, g2, g3, g4, aw,
                  ssem, agaz, agax, agbx, agbz, rsx, rsza, rszb, rsxb, gsem):
    t = Links(ssem, agbx.at[0])
    r, c, x, z = t.r, t.c, t.x, t.z
    xs, zs, qs, cs, send, recv, sent = t.xs, t.zs, t.qs, t.cs, t.send, t.recv, t.sent
    greeted = t.greet([*xs.values(), *(zs[d] for d in (1, 4, 8, 12, 15)), *qs.values(), *cs.values()])

    left = panel[...]
    gram[...] = dot6(left.T, left)
    greeted()

    def gram_rows(xi):
        return pl.ds(pl.multiple_of(32 * c + 8 * xi, 8), 8)

    for d in (1, 2, 3):
        send(gram.at[gram_rows(lax.rem(x + d, NX))], g0.at[d], gsem.at[0, d], xs[d], 2)

    def gram_0():
        total = gram[gram_rows(x), :]
        for d in (1, 2, 3):
            recv(g0.at[d], gsem.at[0, d])
            total = total + g0[d]
        g1[0] = total
        for d in (1, 2, 3):
            send(g1.at[0], g1.at[d], gsem.at[1, d], qs[d], 2)

    def gram_1():
        total = g1[0]
        for d in (1, 2, 3):
            recv(g1.at[d], gsem.at[1, d])
            total = total + g1[d]
        g2[0] = total
        for d in (1, 2, 3):
            send(g2.at[0], g2.at[d], gsem.at[2, d], zs[4 * d], 2)

    def gram_2():
        total = g2[0]
        for d in (1, 2, 3):
            recv(g2.at[d], gsem.at[2, d])
            total = total + g2[d]
        g3[x] = total
        for d in (1, 2, 3):
            send(g3.at[x], g3.at[x], gsem.at[3, d], xs[d], 2)

    def gram_3():
        for d in (1, 2, 3):
            recv(g3.at[lax.rem(x - d + NX, NX)], gsem.at[3, d])
        g4[c] = g3[...]
        for d in range(1, NC):
            send(g4.at[c], g4.at[c], gsem.at[4, d], cs[d], 3)

    def gram_4():
        for d in range(1, NC):
            recv(g4.at[lax.rem(c - d + NC, NC)], gsem.at[4, d])
        aw[...] = g4[...].reshape(RANK, RANK)
        sent(gram.at[pl.ds(0, 96)], 2)
        sent(g4.at[pl.ds(0, NC - 1)], 3)

    sub = lax.broadcasted_iota(jnp.int32, (NB, 128), 0)
    lane = lax.broadcasted_iota(jnp.int32, (NB, 128), 1)
    sub_w = lax.broadcasted_iota(jnp.int32, (NB, RANK), 0)
    lane_w = lax.broadcasted_iota(jnp.int32, (NB, RANK), 1)
    i_all = lax.broadcasted_iota(jnp.int32, (RANK, RANK), 0)
    j_all = lax.broadcasted_iota(jnp.int32, (RANK, RANK), 1)

    def factor_block(k):
        first = pl.multiple_of(NB * k, NB)
        rows = aw[pl.ds(first, NB), :]
        near = jnp.where(k < 4, rows[:, :128], rows[:, 128:])
        near = pltpu.roll(near, lax.rem(128 - NB * lax.rem(k, 4), 128), 1)
        e = jnp.where(lane < NB, near, jnp.where(lane - NB == sub, 1.0, 0.0))
        for j in range(0, NB, 4):
            cols = [jnp.broadcast_to(e[:, j + i:j + i + 1], (NB, 128)) for i in range(4)]
            pivots = [e[j + i:j + i + 1, :] for i in range(4)]
            for i in range(4):
                at = slice(j + i, j + i + 1)
                ratio = jnp.where(sub > j + i, cols[i] * (1.0 / cols[i][at, :]), 0.0)
                for m in range(i + 1, 4):
                    cols[m] = cols[m] - ratio * cols[m][at, :]
                    pivots[m] = pivots[m] - ratio[j + m:j + m + 1, :] * pivots[i]
                e = e - ratio * pivots[i]
        diagonal = jnp.sum(jnp.where(lane == sub, e, 0.0), axis=1, keepdims=True)
        inverse = (e * (1.0 / jnp.sqrt(diagonal)))[:, NB:2 * NB]
        here = (lane_w >= first) & (lane_w < first + NB)
        rows = jnp.where(here, jnp.where(lane_w - first == sub_w, 1.0, 0.0), rows)
        rows = dot6(inverse, rows)
        below = jnp.where(lane_w >= first + NB, rows, 0.0)
        done = (i_all >= first + NB) & (j_all >= first) & (j_all < first + NB)
        aw[...] = jnp.where(done, 0.0, aw[...]) - dot6(below.T, rows)
        aw[pl.ds(first, NB), :] = rows

    lp = split(left)

    def term_step(b, carry):
        h = dot3((thi[block(b), :], tlo[block(b), :]), lp)
        term[pl.ds(2 * BLK * b, BLK, stride=2), :] = h[:, :128]
        term[pl.ds(2 * BLK * b + 1, BLK, stride=2), :] = h[:, 128:]
        pl.when(b == 6)(gram_0)
        return carry

    lax.fori_loop(0, NBLK, term_step, 0)
    gram_1()

    def place(k, carry):
        n = lax.rem(jnp.where(lax.rem(k, 2) == 0, z + 8 - k // 2, jnp.where(k == 15, z, z + 9 + k // 2)), NZ)
        for i in range(NX):
            row = lax.rem(x + i, NX) * NZ + n
            part[i, k] = term[pl.ds(pl.multiple_of(CH * row, 8), CH), :]
        return carry

    lax.fori_loop(0, NZ, place, 0)

    half = CA // 2

    def pair(i, s, lo=0, size=CA):
        return part.at[i, pl.ds(2 * s, 2), pl.ds(lo, size)]

    def send_half(s):
        send(pair(2, s, 0, half), xh.at[0, s], rsx.at[0, s], xs[1], 4)
        send(pair(2, s, half, half), xh.at[1, s], rsx.at[1, s], xs[3], 4)

    def send_full(s):
        two = pl.ds(2 * s, 2)
        recv(xh.at[0, s], rsx.at[0, s])
        part[1, two, :half, :] += xh[0, s]
        send(pair(1, s), xf.at[0, s], rsx.at[2, s], xs[1], 4)
        recv(xh.at[1, s], rsx.at[1, s])
        part[3, two, half:CA, :] += xh[1, s]
        send(pair(3, s), xf.at[1, s], rsx.at[3, s], xs[3], 4)

    def take_full(s):
        two = pl.ds(2 * s, 2)
        recv(xf.at[0, s], rsx.at[2, s])
        recv(xf.at[1, s], rsx.at[3, s])
        part[0, two, :CA, :] += xf[0, s] + xf[1, s]

    send_half(0)
    send_half(1)
    send_full(0)

    def reduce_step(s, carry):
        @pl.when(s < 6)
        def _():
            send_half(s + 2)

        for i, g in enumerate((1, 0)):
            rows = pl.ds(2 * g, 2)
            kl, kr = jnp.maximum(2 * s - 1, 0), 2 * s + 2

            @pl.when(s > 0)
            def _():
                recv(zb.at[1, i, s], rszb.at[1, i, s])
                part[rows, kl, CA:, :] += zb[1, i, s]

            send(part.at[rows, kl, pl.ds(CA, CB)], zb.at[1, i, s + 1], rszb.at[1, i, s + 1], zs[15], 4)

            @pl.when(s < 7)
            def _():
                @pl.when(s > 0)
                def _():
                    recv(zb.at[0, i, s], rszb.at[0, i, s])
                    part[rows, kr, CA:, :] += zb[0, i, s]

                send(part.at[rows, kr, pl.ds(CA, CB)], zb.at[0, i, s + 1], rszb.at[0, i, s + 1], zs[1], 4)

        @pl.when(s < 7)
        def _():
            send_full(s + 1)

        take_full(s)

        @pl.when(s > 0)
        def _():
            recv(za.at[0, s], rsza.at[0, s])
            part[0, 2 * s, :CA, :] += za[0, s]

        send(part.at[0, 2 * s, pl.ds(0, CA)], za.at[0, s + 1], rsza.at[0, s + 1], zs[1], 4)

        @pl.when(s < 7)
        def _():
            @pl.when(s > 0)
            def _():
                recv(za.at[1, s], rsza.at[1, s])
                part[0, 2 * s + 1, :CA, :] += za[1, s]

            send(part.at[0, 2 * s + 1, pl.ds(0, CA)], za.at[1, s + 1], rsza.at[1, s + 1], zs[15], 4)

        for when, stage in enumerate((gram_2, gram_3, gram_4)):
            pl.when(s == when)(stage)

        @pl.when(s > 2)
        def _():
            factor_block(s - 3)

        return carry

    lax.fori_loop(0, 8, reduce_step, 0)
    for i, g in enumerate((1, 0)):
        recv(zb.at[1, i, 8], rszb.at[1, i, 8])
        recv(zb.at[0, i, 7], rszb.at[0, i, 7])
        part[2 * g:2 * g + 2, 15, CA:, :] += zb[1, i, 8] + zb[0, i, 7]
    for d in (1, 2, 3):
        send(part.at[d, 15, pl.ds(CA, CB)], xb.at[d], rsxb.at[d], xs[d], 4)
    recv(za.at[0, 8], rsza.at[0, 8])
    recv(za.at[1, 7], rsza.at[1, 7])
    red[0, 0, :CA, :] = part[0, 15, :CA, :] + (za[0, 8] + za[1, 7])
    total = part[0, 15, CA:, :]
    for d in (1, 2, 3):
        recv(xb.at[d], rsxb.at[d])
        total = total + xb[d]
    red[0, 0, CA:, :] = total
    sent(term.at[pl.ds(0, 6552)], 4)

    def factor_rest(s):
        @pl.when(s < 4)
        def _():
            factor_block(s + 4)

    gather(t, red, red2, (agaz, agax, agbx, agbz), factor_rest)
    lower[...] = jnp.where(i_all >= j_all, aw[...], 0.0)
    own[...] = red[0, 0]


def scale_kernel(panel, red2, lower, own, rfh, rfl, basis, update, ownf, rfhv, rflv, sq, sqr,
                 ssem, qsem, osem, *, n_cols, scale):
    t = Links(ssem, qsem.at[0])
    cs, send, recv, sent = t.cs, t.send, t.recv, t.sent
    greeted = t.greet(cs.values())

    inverse = lower[...]
    nt = ((1,), (1,))
    inv = split(inverse)

    def right_step(b, squares):
        rf = dot3(split_rows(red2, b), inv, nt)
        rfhv[block(b), :], rflv[block(b), :] = split(rf)
        return squares + jnp.sum((rf * rf).reshape(BLK // 8, 8, RANK), axis=0)

    squares = lax.fori_loop(0, NBLK, right_step, jnp.zeros((8, RANK), F32))
    stores = (pltpu.make_async_copy(rfhv, rfh, osem.at[0]), pltpu.make_async_copy(rflv, rfl, osem.at[1]))
    for store in stores:
        store.start()
    sq[...] = squares
    greeted()
    for d in range(1, NC):
        send(sq, sqr.at[d], qsem.at[d], cs[d], 0)
    left_basis = dot6(panel[...], inverse, nt)
    halves = [own[pl.ds(h, CH // 2, stride=2), :] for h in (0, 1)]
    own_rf = dot6(jnp.concatenate(halves, axis=1), inverse, nt)
    for d in range(1, NC):
        recv(sqr.at[d], qsem.at[d])
        squares = squares + sqr[d]
    rms = jnp.sqrt(jnp.sum(squares, axis=0, keepdims=True) * (1.0 / n_cols) + EPSILON)
    ownf[...] = own_rf / rms
    basis[...] = left_basis * -(1.0 - MOMENTUM_KEEP)
    update[...] = left_basis * (-scale / rms)
    sent(sqr.at[pl.ds(0, NC - 1)], 0)
    for store in stores:
        store.wait()


def output_kernel(mom, grad, rfh, rfl, basis, update, ownf, momo, wupd, faco):
    nt = ((1,), (1,))
    high, low = split(update[...])
    rows = jnp.concatenate([basis[...].astype(BF16), high, low], axis=0)
    for first in range(0, HALF, BLK):
        at = slice(first, min(first + BLK, HALF))
        product = dot(rows, rfh[at, :], nt)
        momo[:, at] = mom[:, at] + grad[:, at].astype(F32) + product[:ROWS]
        wupd[:, at] = (product[ROWS:2 * ROWS] + (product[2 * ROWS:] + dot(high, rfl[at, :], nt))).astype(BF16)

    @pl.when(pl.program_id(0) == 0)
    def _():
        faco[...] = ownf[...]


def shards(momentum, gradient, factor):
    rows = momentum.shape[0] * lax.axis_size("row")
    n_cols = momentum.shape[1] * lax.axis_size("col")
    scale = STEP_SIZE * math.sqrt(rows / factor.shape[1])
    dma, vmem, hbm = pltpu.SemaphoreType.DMA, pltpu.VMEM, pl.BlockSpec(memory_space=pl.ANY)
    inside = pl.BlockSpec(memory_space=pltpu.VMEM)
    shape = jax.ShapeDtypeStruct
    flat, natural = vmem((NX, NZ, CH, 128), F32), vmem((NX * NZ * CH, 128), F32)
    gather_sems = [dma((2, 9)), dma((4, 9)), dma((4,)), dma((2, 2, 9))]

    def call(body, name, collective, inputs, outputs, scratch):
        return pl.pallas_call(
            body, name=name, out_shape=tuple(o[0] for o in outputs), out_specs=tuple(o[1] for o in outputs),
            in_specs=[i[1] for i in inputs], scratch_shapes=scratch,
            compiler_params=pltpu.CompilerParams(
                collective_id=collective, has_side_effects=True, vmem_limit_bytes=60 * 2**20),
        )(*(i[0] for i in inputs))

    narrow, tall = (shape((ROWS, COLS), BF16), inside), (shape((COLS, ROWS), BF16), inside)
    gathered = (shape((NX * NZ * CH, 128), F32), inside)
    square, chunk = (shape((RANK, RANK), F32), inside), (shape((CH, 128), F32), inside)
    gat, bhi, blo, thi, tlo = call(
        gather_kernel, "gather_factor", 0, [(momentum, hbm), (gradient, hbm), (factor, inside)],
        [gathered, narrow, narrow, tall, tall],
        [vmem((ROWS, COLS), F32), vmem((ROWS, COLS), BF16), flat, dma((2,)), dma((1,)), *gather_sems])
    rows16 = vmem((NC, ROWS // NC, RANK), F32)
    (panel,) = call(
        panel_kernel, "left_panel", 1, [(gat, inside), (bhi, inside), (blo, inside)],
        [(shape((NC, ROWS // NC, RANK), F32), inside)], [rows16, rows16, dma((1,)), dma((2, NC))])
    panel = panel.reshape(ROWS, RANK)
    small = vmem((4, 8, RANK), F32)
    red, lower, own = call(
        factor_kernel, "sum_and_factor", 2, [(panel, inside), (thi, inside), (tlo, inside)],
        [gathered, square, chunk],
        [natural, flat, flat, vmem((2, 8, 2, CA // 2, 128), F32), vmem((2, 8, 2, CA, 128), F32),
         vmem((2, 9, CA, 128), F32), vmem((2, 2, 9, 2, CB, 128), F32), vmem((4, CB, 128), F32),
         vmem((RANK, RANK), F32), small, small, small, small, vmem((NC, 4, 8, RANK), F32), vmem((RANK, RANK), F32),
         dma((7,)), *gather_sems, dma((4, 8)), dma((2, 9)), dma((2, 2, 9)), dma((4,)), dma((5, NC))])
    half_right = (shape((COLS, RANK), BF16), hbm)
    thin = (shape((ROWS, RANK), F32), inside)
    rfh, rfl, basis, update, ownf = call(
        functools.partial(scale_kernel, n_cols=n_cols, scale=scale), "right_factor", 3,
        [(panel, inside), (red, inside), (lower, inside), (own, inside)],
        [half_right, half_right, thin, thin, (shape((CH // 2, RANK), F32), inside)],
        [vmem((COLS, RANK), BF16), vmem((COLS, RANK), BF16), vmem((8, RANK), F32), vmem((NC, 8, RANK), F32),
         dma((1,)), dma((NC,)), dma((2,))])
    whole = pl.BlockSpec((ROWS, RANK), lambda b: (0, 0))
    across = pl.BlockSpec((ROWS, HALF), lambda b: (0, b))
    down = pl.BlockSpec((HALF, RANK), lambda b: (b, 0))
    chunk = pl.BlockSpec((CH // 2, RANK), lambda b: (0, 0))
    return pl.pallas_call(
        output_kernel,
        grid=(2,),
        out_shape=(shape((ROWS, COLS), F32), shape((ROWS, COLS), BF16), shape((CH // 2, RANK), F32)),
        in_specs=[across, across, down, down, whole, whole, chunk],
        out_specs=(across, across, chunk),
        compiler_params=pltpu.CompilerParams(vmem_limit_bytes=60 * 2**20),
        name="outputs",
    )(momentum, gradient, rfh, rfl, basis, update, ownf)


def solution(mesh):
    placed = (P("row", "col"), P("row", "col"), P(("col", "row"), None))
    return jax.shard_map(shards, mesh=mesh, in_specs=placed, out_specs=placed, check_vma=False)
```

```python
import functools
import math

import jax
import jax.numpy as jnp
from jax import lax
from jax.experimental import pallas as pl
from jax.experimental.pallas import tpu as pltpu
from jax.sharding import PartitionSpec as P

HIGHEST = lax.Precision.HIGHEST
MOMENTUM_KEEP = 0.8
STEP_SIZE = 0.3
EPSILON = 1e-06
F32 = jnp.float32
BF16 = jnp.bfloat16

NX, NZ = 4, 16
NC = 8
CH = 104
CA = 64
CB = CH - CA
ROWS, COLS, RANK = 128, 3328, 256
BLK = 256
NBLK = COLS // BLK
HALF = COLS // 2
NB = 32


def split(value):
    high = value.astype(BF16)
    return high, (value - high.astype(F32)).astype(BF16)


def dot(a, b, dims=((1,), (0,))):
    return lax.dot_general(a, b, (dims, ((), ())), preferred_element_type=F32)


def dot3(a, b, dims=((1,), (0,))):
    return dot(a[0], b[0], dims) + (dot(a[0], b[1], dims) + dot(a[1], b[0], dims))


def dot6(a, b, dims=((1,), (0,))):
    return lax.dot_general(a, b, (dims, ((), ())), precision=HIGHEST, preferred_element_type=F32)


class Links:
    def __init__(self, ssem, rsem):
        self.ssem, self.rsem = ssem, rsem
        self.r, self.c = lax.axis_index("row"), lax.axis_index("col")
        self.x, self.z = self.r // NZ, self.r % NZ

        x, z, c = self.x, self.z, self.c
        self.xs = {d: {"row": lax.rem(x + d, NX) * NZ + z, "col": c} for d in (1, 2, 3)}
        self.zs = {d: {"row": x * NZ + lax.rem(z + d, NZ), "col": c} for d in (1, 4, 8, 12, 15)}
        self.qs = {d: {"row": x * NZ + (z // 4) * 4 + lax.rem(z + d, 4), "col": c} for d in (1, 2, 3)}
        self.cs = {d: {"row": self.r, "col": lax.rem(c + d, NC)} for d in range(1, NC)}

    def copy(self, src, dst, recv, device, slot=0):
        return pltpu.make_async_remote_copy(
            src_ref=src, dst_ref=dst, send_sem=self.ssem.at[slot], recv_sem=recv,
            device_id=device, device_id_type=pl.DeviceIdType.MESH)

    def send(self, src, dst, recv, device, slot):
        self.copy(src, dst, recv, device, slot).start()

    def recv(self, dst, sem):
        self.copy(dst, dst, sem, self.xs[1]).wait_recv()

    def sent(self, ref, slot):
        self.copy(ref, ref, self.rsem, self.xs[1], slot).wait_send()

    def greet(self, peers):
        barrier = pltpu.get_barrier_semaphore()
        for peer in peers:
            pl.semaphore_signal(barrier, inc=1, device_id=peer, device_id_type=pl.DeviceIdType.MESH)
        return lambda: pl.semaphore_wait(barrier, len(peers))


def block(b):
    return pl.ds(pl.multiple_of(b * BLK, BLK), BLK)


def split_rows(ref, b):
    parts = [split(ref[pl.ds(2 * BLK * b + h, BLK, stride=2), :]) for h in (0, 1)]
    return tuple(jnp.concatenate(p, axis=1) for p in zip(*parts))


def gather(t, buf, natural, sems, work):
    agaz, agax, agbx, agbz = sems
    xs, send, recv = t.xs, t.send, t.recv
    right, left = t.zs[1], t.zs[15]
    half = CA // 2

    def one(k):
        return buf.at[0, k, pl.ds(0, CA)]

    def two(i, k, n, lo=0, size=CA):
        return buf.at[i, pl.ds(k, n), pl.ds(lo, size)]

    def group(g, k):
        return buf.at[pl.ds(2 * g, 2), k, pl.ds(CA, CB)]

    def side(k, n, s):
        send(two(0, k, n), two(1, k, n), agax.at[0, s], xs[1], 0)
        send(two(0, k, n), two(3, k, n), agax.at[1, s], xs[3], 0)

    def forward(k, n, s):
        recv(two(1, k, n), agax.at[0, s])
        send(two(1, k, n, 0, half), two(2, k, n, 0, half), agax.at[2, s], xs[1], 0)
        recv(two(3, k, n), agax.at[1, s])
        send(two(3, k, n, half, half), two(2, k, n, half, half), agax.at[3, s], xs[3], 0)

    def finish(k, n, s):
        recv(two(2, k, n, 0, half), agax.at[2, s])
        recv(two(2, k, n, half, half), agax.at[3, s])

    for d in (1, 2, 3):
        send(buf.at[0, 0, pl.ds(CA, CB)], buf.at[d, 0, pl.ds(CA, CB)], agbx.at[d], xs[d], 0)
    send(one(0), one(1), agaz.at[0, 1], right, 0)
    send(one(0), one(2), agaz.at[1, 1], left, 0)
    side(0, 1, 0)
    for d in (1, 2, 3):
        recv(buf.at[d, 0, pl.ds(CA, CB)], agbx.at[d])
    for g in (0, 1):
        send(group(g, 0), group(g, 1), agbz.at[0, g, 1], right, 0)
        send(group(g, 0), group(g, 2), agbz.at[1, g, 1], left, 0)
    forward(0, 1, 0)

    def step(s, carry):
        kr, kl = 2 * s - 1, 2 * s
        recv(one(kr), agaz.at[0, s])
        send(one(kr), one(kr + 2), agaz.at[0, s + 1], right, 0)
        recv(one(kl), agaz.at[1, s])

        @pl.when(s < 7)
        def _():
            send(one(kl), one(kl + 2), agaz.at[1, s + 1], left, 0)

        side(kr, 2, s)
        for g in (0, 1):
            recv(group(g, kl), agbz.at[1, g, s])
            send(group(g, kl), group(g, jnp.minimum(kl + 2, 15)), agbz.at[1, g, s + 1], left, 0)
            recv(group(g, kr), agbz.at[0, g, s])

            @pl.when(s < 7)
            def _():
                send(group(g, kr), group(g, kr + 2), agbz.at[0, g, s + 1], right, 0)

        @pl.when(s > 1)
        def _():
            forward(kr - 2, 2, s - 1)

        work(s)
        return carry

    lax.fori_loop(1, 8, step, 0)
    recv(one(15), agaz.at[0, 8])
    side(15, 1, 8)
    forward(13, 2, 7)
    for g in (0, 1):
        recv(group(g, 15), agbz.at[1, g, 8])
    forward(15, 1, 8)
    finish(0, 1, 0)

    def last(s, carry):
        finish(2 * s - 1, 2, s)
        return carry

    lax.fori_loop(1, 8, last, 0)
    finish(15, 1, 8)
    t.sent(buf.reshape(NX * NZ * CH, 128).at[pl.ds(0, 6552)], 0)

    def place(n, carry):
        s = lax.rem(t.z - n + 2 * NZ, NZ)
        k = jnp.where(s == 0, 0, jnp.where(s > 8, 2 * (NZ - s), 2 * s - 1))
        for i in range(NX):
            row = lax.rem(t.x - i + NX, NX) * NZ + n
            natural[pl.ds(pl.multiple_of(CH * row, 8), CH), :] = buf[i, k]
        return carry

    lax.fori_loop(0, NZ, place, 0)


def panel_kernel(mom, grad, fac, panel, thi, tlo, momv, gradv, bhi, blo, gat, gat2, ppart, precv,
                 lsem, ssem, agaz, agax, agbx, agbz, psem):
    t = Links(ssem, agbx.at[0])
    c, cs, send, recv, sent = t.c, t.cs, t.send, t.recv, t.sent
    loads = (pltpu.make_async_copy(mom, momv, lsem.at[0]), pltpu.make_async_copy(grad, gradv, lsem.at[1]))
    for load in loads:
        load.start()
    greeted = t.greet([*t.xs.values(), *cs.values(), t.zs[1], t.zs[15]])

    gat.at[0, 0][pl.ds(0, CH // 2, stride=2), :] = fac[:, :128]
    gat.at[0, 0][pl.ds(1, CH // 2, stride=2), :] = fac[:, 128:]
    greeted()

    def prepare(b):
        at = block(b)
        value = momv[:, at] + gradv[:, at].astype(F32)
        high, low = split(value)
        bhi[:, at], blo[:, at] = high, low
        high, low = split(value.T)
        thi[at, :], tlo[at, :] = high, low

    def prepare_step(s):
        @pl.when(s == 1)
        def _():
            for load in loads:
                load.wait()

        prepare(2 * s - 2)

        @pl.when(s < 7)
        def _():
            prepare(2 * s - 1)

    gather(t, gat, gat2, (agaz, agax, agbx, agbz), prepare_step)

    def panel_step(b, total):
        at = block(b)
        return total + dot3((bhi[:, at], blo[:, at]), split_rows(gat2, b))

    total = lax.fori_loop(0, NBLK, panel_step, jnp.zeros((ROWS, RANK), F32))
    ppart[...] = total.reshape(NC, ROWS // NC, RANK)
    for d in range(1, NC):
        send(ppart.at[cs[d]["col"]], precv.at[d], psem.at[0, d], cs[d], 1)
    mine = ppart[c]
    for d in range(1, NC):
        recv(precv.at[d], psem.at[0, d])
        mine = mine + precv[d]
    panel[c] = mine
    for d in range(1, NC):
        send(panel.at[c], panel.at[c], psem.at[1, d], cs[d], 1)
    for d in range(1, NC):
        recv(panel.at[lax.rem(c - d + NC, NC)], psem.at[1, d])
    sent(gat2.at[pl.ds(0, 14 * 32)], 1)


def factor_kernel(panel, thi, tlo, rfh, rfl, basis, update, ownf,
                  term, part, red, red2, xh, xf, za, zb, xb, gram, g0, g1, g2, g3, g4, aw, rfhv, rflv, sq, sqr,
                  ssem, agaz, agax, agbx, agbz, rsx, rsza, rszb, rsxb, gsem, qsem, osem, *, n_cols, scale):
    t = Links(ssem, agbx.at[0])
    r, c, x, z = t.r, t.c, t.x, t.z
    xs, zs, qs, cs, send, recv, sent = t.xs, t.zs, t.qs, t.cs, t.send, t.recv, t.sent
    greeted = t.greet([*xs.values(), *zs.values(), *qs.values(), *cs.values()])

    left = panel[...]
    gram[...] = dot6(left.T, left)
    greeted()

    def gram_rows(xi):
        return pl.ds(pl.multiple_of(32 * c + 8 * xi, 8), 8)

    for d in (1, 2, 3):
        send(gram.at[gram_rows(lax.rem(x + d, NX))], g0.at[d], gsem.at[0, d], xs[d], 2)

    def gram_0():
        total = gram[gram_rows(x), :]
        for d in (1, 2, 3):
            recv(g0.at[d], gsem.at[0, d])
            total = total + g0[d]
        g1[0] = total
        for d in (1, 2, 3):
            send(g1.at[0], g1.at[d], gsem.at[1, d], qs[d], 2)

    def gram_1():
        total = g1[0]
        for d in (1, 2, 3):
            recv(g1.at[d], gsem.at[1, d])
            total = total + g1[d]
        g2[0] = total
        for d in (1, 2, 3):
            send(g2.at[0], g2.at[d], gsem.at[2, d], zs[4 * d], 2)

    def gram_2():
        total = g2[0]
        for d in (1, 2, 3):
            recv(g2.at[d], gsem.at[2, d])
            total = total + g2[d]
        g3[x] = total
        for d in (1, 2, 3):
            send(g3.at[x], g3.at[x], gsem.at[3, d], xs[d], 2)

    def gram_3():
        for d in (1, 2, 3):
            recv(g3.at[lax.rem(x - d + NX, NX)], gsem.at[3, d])
        g4[c] = g3[...]
        for d in range(1, NC):
            send(g4.at[c], g4.at[c], gsem.at[4, d], cs[d], 3)

    def gram_4():
        for d in range(1, NC):
            recv(g4.at[lax.rem(c - d + NC, NC)], gsem.at[4, d])
        aw[...] = g4[...].reshape(RANK, RANK)
        sent(gram.at[pl.ds(0, 96)], 2)
        sent(g4.at[pl.ds(0, NC - 1)], 3)

    sub = lax.broadcasted_iota(jnp.int32, (NB, 128), 0)
    lane = lax.broadcasted_iota(jnp.int32, (NB, 128), 1)
    sub_w = lax.broadcasted_iota(jnp.int32, (NB, RANK), 0)
    lane_w = lax.broadcasted_iota(jnp.int32, (NB, RANK), 1)
    i_all = lax.broadcasted_iota(jnp.int32, (RANK, RANK), 0)
    j_all = lax.broadcasted_iota(jnp.int32, (RANK, RANK), 1)

    def factor_block(k):
        first = pl.multiple_of(NB * k, NB)
        rows = aw[pl.ds(first, NB), :]
        near = jnp.where(k < 4, rows[:, :128], rows[:, 128:])
        near = pltpu.roll(near, lax.rem(128 - NB * lax.rem(k, 4), 128), 1)
        e = jnp.where(lane < NB, near, jnp.where(lane - NB == sub, 1.0, 0.0))
        for j in range(0, NB, 4):
            cols = [jnp.broadcast_to(e[:, j + i:j + i + 1], (NB, 128)) for i in range(4)]
            pivots = [e[j + i:j + i + 1, :] for i in range(4)]
            for i in range(4):
                at = slice(j + i, j + i + 1)
                ratio = jnp.where(sub > j + i, cols[i] * (1.0 / cols[i][at, :]), 0.0)
                for m in range(i + 1, 4):
                    cols[m] = cols[m] - ratio * cols[m][at, :]
                    pivots[m] = pivots[m] - ratio[j + m:j + m + 1, :] * pivots[i]
                e = e - ratio * pivots[i]
        diagonal = jnp.sum(jnp.where(lane == sub, e, 0.0), axis=1, keepdims=True)
        inverse = (e * (1.0 / jnp.sqrt(diagonal)))[:, NB:2 * NB]
        here = (lane_w >= first) & (lane_w < first + NB)
        rows = jnp.where(here, jnp.where(lane_w - first == sub_w, 1.0, 0.0), rows)
        rows = dot6(inverse, rows)
        below = jnp.where(lane_w >= first + NB, rows, 0.0)
        done = (i_all >= first + NB) & (j_all >= first) & (j_all < first + NB)
        aw[...] = jnp.where(done, 0.0, aw[...]) - dot6(below.T, rows)
        aw[pl.ds(first, NB), :] = rows

    lp = split(left)

    def term_step(b, carry):
        h = dot3((thi[block(b), :], tlo[block(b), :]), lp)
        term[pl.ds(2 * BLK * b, BLK, stride=2), :] = h[:, :128]
        term[pl.ds(2 * BLK * b + 1, BLK, stride=2), :] = h[:, 128:]
        pl.when(b == 6)(gram_0)
        return carry

    lax.fori_loop(0, NBLK, term_step, 0)
    gram_1()

    def place(k, carry):
        n = lax.rem(jnp.where(lax.rem(k, 2) == 0, z + 8 - k // 2, jnp.where(k == 15, z, z + 9 + k // 2)), NZ)
        for i in range(NX):
            row = lax.rem(x + i, NX) * NZ + n
            part[i, k] = term[pl.ds(pl.multiple_of(CH * row, 8), CH), :]
        return carry

    lax.fori_loop(0, NZ, place, 0)

    half = CA // 2

    def pair(i, s, lo=0, size=CA):
        return part.at[i, pl.ds(2 * s, 2), pl.ds(lo, size)]

    def send_half(s):
        send(pair(2, s, 0, half), xh.at[0, s], rsx.at[0, s], xs[1], 4)
        send(pair(2, s, half, half), xh.at[1, s], rsx.at[1, s], xs[3], 4)

    def send_full(s):
        two = pl.ds(2 * s, 2)
        recv(xh.at[0, s], rsx.at[0, s])
        part[1, two, :half, :] += xh[0, s]
        send(pair(1, s), xf.at[0, s], rsx.at[2, s], xs[1], 4)
        recv(xh.at[1, s], rsx.at[1, s])
        part[3, two, half:CA, :] += xh[1, s]
        send(pair(3, s), xf.at[1, s], rsx.at[3, s], xs[3], 4)

    def take_full(s):
        two = pl.ds(2 * s, 2)
        recv(xf.at[0, s], rsx.at[2, s])
        recv(xf.at[1, s], rsx.at[3, s])
        part[0, two, :CA, :] += xf[0, s] + xf[1, s]

    send_half(0)
    send_half(1)
    send_full(0)

    def reduce_step(s, carry):
        @pl.when(s < 6)
        def _():
            send_half(s + 2)

        for i, g in enumerate((1, 0)):
            rows = pl.ds(2 * g, 2)
            kl, kr = jnp.maximum(2 * s - 1, 0), 2 * s + 2

            @pl.when(s > 0)
            def _():
                recv(zb.at[1, i, s], rszb.at[1, i, s])
                part[rows, kl, CA:, :] += zb[1, i, s]

            send(part.at[rows, kl, pl.ds(CA, CB)], zb.at[1, i, s + 1], rszb.at[1, i, s + 1], zs[15], 4)

            @pl.when(s < 7)
            def _():
                @pl.when(s > 0)
                def _():
                    recv(zb.at[0, i, s], rszb.at[0, i, s])
                    part[rows, kr, CA:, :] += zb[0, i, s]

                send(part.at[rows, kr, pl.ds(CA, CB)], zb.at[0, i, s + 1], rszb.at[0, i, s + 1], zs[1], 4)

        @pl.when(s < 7)
        def _():
            send_full(s + 1)

        take_full(s)

        @pl.when(s > 0)
        def _():
            recv(za.at[0, s], rsza.at[0, s])
            part[0, 2 * s, :CA, :] += za[0, s]

        send(part.at[0, 2 * s, pl.ds(0, CA)], za.at[0, s + 1], rsza.at[0, s + 1], zs[1], 4)

        @pl.when(s < 7)
        def _():
            @pl.when(s > 0)
            def _():
                recv(za.at[1, s], rsza.at[1, s])
                part[0, 2 * s + 1, :CA, :] += za[1, s]

            send(part.at[0, 2 * s + 1, pl.ds(0, CA)], za.at[1, s + 1], rsza.at[1, s + 1], zs[15], 4)

        for when, stage in enumerate((gram_2, gram_3, gram_4)):
            pl.when(s == when)(stage)

        @pl.when(s > 2)
        def _():
            factor_block(s - 3)

        return carry

    lax.fori_loop(0, 8, reduce_step, 0)
    for i, g in enumerate((1, 0)):
        recv(zb.at[1, i, 8], rszb.at[1, i, 8])
        recv(zb.at[0, i, 7], rszb.at[0, i, 7])
        part[2 * g:2 * g + 2, 15, CA:, :] += zb[1, i, 8] + zb[0, i, 7]
    for d in (1, 2, 3):
        send(part.at[d, 15, pl.ds(CA, CB)], xb.at[d], rsxb.at[d], xs[d], 4)
    recv(za.at[0, 8], rsza.at[0, 8])
    recv(za.at[1, 7], rsza.at[1, 7])
    red[0, 0, :CA, :] = part[0, 15, :CA, :] + (za[0, 8] + za[1, 7])
    total = part[0, 15, CA:, :]
    for d in (1, 2, 3):
        recv(xb.at[d], rsxb.at[d])
        total = total + xb[d]
    red[0, 0, CA:, :] = total
    sent(term.at[pl.ds(0, 6552)], 4)

    def factor_rest(s):
        @pl.when(s < 4)
        def _():
            factor_block(s + 4)

    gather(t, red, red2, (agaz, agax, agbx, agbz), factor_rest)

    inverse = jnp.where(i_all >= j_all, aw[...], 0.0)
    nt = ((1,), (1,))
    inv = split(inverse)

    def right_step(b, squares):
        rf = dot3(split_rows(red2, b), inv, nt)
        rfhv[block(b), :], rflv[block(b), :] = split(rf)
        return squares + jnp.sum((rf * rf).reshape(BLK // 8, 8, RANK), axis=0)

    squares = lax.fori_loop(0, NBLK, right_step, jnp.zeros((8, RANK), F32))
    stores = (pltpu.make_async_copy(rfhv, rfh, osem.at[0]), pltpu.make_async_copy(rflv, rfl, osem.at[1]))
    for store in stores:
        store.start()
    sq[...] = squares
    for d in range(1, NC):
        send(sq, sqr.at[d], qsem.at[d], cs[d], 6)
    left_basis = dot6(left, inverse, nt)
    halves = [red.at[0, 0][pl.ds(h, CH // 2, stride=2), :] for h in (0, 1)]
    own_rf = dot6(jnp.concatenate(halves, axis=1), inverse, nt)
    for d in range(1, NC):
        recv(sqr.at[d], qsem.at[d])
        squares = squares + sqr[d]
    rms = jnp.sqrt(jnp.sum(squares, axis=0, keepdims=True) * (1.0 / n_cols) + EPSILON)
    ownf[...] = own_rf / rms
    basis[...] = left_basis * -(1.0 - MOMENTUM_KEEP)
    update[...] = left_basis * (-scale / rms)
    sent(gram.at[pl.ds(0, 8 * (NC - 1))], 6)
    for store in stores:
        store.wait()


def output_kernel(mom, grad, rfh, rfl, basis, update, ownf, momo, wupd, faco):
    nt = ((1,), (1,))
    high, low = split(update[...])
    rows = jnp.concatenate([basis[...].astype(BF16), high, low], axis=0)
    for first in range(0, HALF, BLK):
        at = slice(first, min(first + BLK, HALF))
        product = dot(rows, rfh[at, :], nt)
        momo[:, at] = mom[:, at] + grad[:, at].astype(F32) + product[:ROWS]
        wupd[:, at] = (product[ROWS:2 * ROWS] + (product[2 * ROWS:] + dot(high, rfl[at, :], nt))).astype(BF16)

    @pl.when(pl.program_id(0) == 0)
    def _():
        faco[...] = ownf[...]


def shards(momentum, gradient, factor):
    rows = momentum.shape[0] * lax.axis_size("row")
    n_cols = momentum.shape[1] * lax.axis_size("col")
    scale = STEP_SIZE * math.sqrt(rows / factor.shape[1])
    dma, vmem, hbm = pltpu.SemaphoreType.DMA, pltpu.VMEM, pl.BlockSpec(memory_space=pl.ANY)
    inside = pl.BlockSpec(memory_space=pltpu.VMEM)
    shape = jax.ShapeDtypeStruct
    flat, natural = vmem((NX, NZ, CH, 128), F32), vmem((NX * NZ * CH, 128), F32)
    gather_sems = [dma((2, 9)), dma((4, 9)), dma((4,)), dma((2, 2, 9))]
    rows16 = vmem((NC, ROWS // NC, RANK), F32)
    panel, thi, tlo = pl.pallas_call(
        panel_kernel,
        out_shape=(shape((NC, ROWS // NC, RANK), F32), shape((COLS, ROWS), BF16), shape((COLS, ROWS), BF16)),
        in_specs=[hbm, hbm, inside],
        out_specs=(inside, inside, inside),
        scratch_shapes=[
            vmem((ROWS, COLS), F32), vmem((ROWS, COLS), BF16), vmem((ROWS, COLS), BF16), vmem((ROWS, COLS), BF16),
            flat, natural, rows16, rows16, dma((2,)), dma((2,)), *gather_sems, dma((2, NC)),
        ],
        compiler_params=pltpu.CompilerParams(collective_id=0, has_side_effects=True, vmem_limit_bytes=60 * 2**20),
        name="left_panel",
    )(momentum, gradient, factor)
    small = vmem((4, 8, RANK), F32)
    rfh, rfl, basis, update, ownf = pl.pallas_call(
        functools.partial(factor_kernel, n_cols=n_cols, scale=scale),
        out_shape=(
            shape((COLS, RANK), BF16), shape((COLS, RANK), BF16),
            shape((ROWS, RANK), F32), shape((ROWS, RANK), F32), shape((CH // 2, RANK), F32)),
        in_specs=[inside, inside, inside],
        out_specs=(hbm, hbm, inside, inside, inside),
        scratch_shapes=[
            natural, flat, flat, natural, vmem((2, 8, 2, CA // 2, 128), F32), vmem((2, 8, 2, CA, 128), F32),
            vmem((2, 9, CA, 128), F32), vmem((2, 2, 9, 2, CB, 128), F32), vmem((4, CB, 128), F32),
            vmem((RANK, RANK), F32), small, small, small, small, vmem((NC, 4, 8, RANK), F32),
            vmem((RANK, RANK), F32), vmem((COLS, RANK), BF16), vmem((COLS, RANK), BF16),
            vmem((8, RANK), F32), vmem((NC, 8, RANK), F32),
            dma((7,)), *gather_sems, dma((4, 8)), dma((2, 9)), dma((2, 2, 9)), dma((4,)),
            dma((5, NC)), dma((NC,)), dma((2,)),
        ],
        compiler_params=pltpu.CompilerParams(collective_id=1, has_side_effects=True, vmem_limit_bytes=60 * 2**20),
        name="right_factor",
    )(panel.reshape(ROWS, RANK), thi, tlo)
    whole = pl.BlockSpec((ROWS, RANK), lambda b: (0, 0))
    across = pl.BlockSpec((ROWS, HALF), lambda b: (0, b))
    down = pl.BlockSpec((HALF, RANK), lambda b: (b, 0))
    chunk = pl.BlockSpec((CH // 2, RANK), lambda b: (0, 0))
    return pl.pallas_call(
        output_kernel,
        grid=(2,),
        out_shape=(shape((ROWS, COLS), F32), shape((ROWS, COLS), BF16), shape((CH // 2, RANK), F32)),
        in_specs=[across, across, down, down, whole, whole, chunk],
        out_specs=(across, across, chunk),
        compiler_params=pltpu.CompilerParams(vmem_limit_bytes=60 * 2**20),
        name="outputs",
    )(momentum, gradient, rfh, rfl, basis, update, ownf)


def solution(mesh):
    placed = (P("row", "col"), P("row", "col"), P(("col", "row"), None))
    return jax.shard_map(shards, mesh=mesh, in_specs=placed, out_specs=placed, check_vma=False)
```

```python
import functools
import math

import jax
import jax.numpy as jnp
from jax import lax
from jax.experimental import pallas as pl
from jax.experimental.pallas import tpu as pltpu
from jax.sharding import PartitionSpec as P

HIGHEST = lax.Precision.HIGHEST
MOMENTUM_KEEP = 0.8
STEP_SIZE = 0.3
EPSILON = 1e-06
F32 = jnp.float32
BF16 = jnp.bfloat16

NX, NZ = 4, 16
NC = 8
CH = 104
CA = 64
CB = CH - CA
ROWS, COLS, RANK = 128, 3328, 256
BLK = 256
NBLK = COLS // BLK
HALF = COLS // 2
NB = 32


def split(value):
    high = value.astype(BF16)
    return high, (value - high.astype(F32)).astype(BF16)


def dot(a, b, dims=((1,), (0,))):
    return lax.dot_general(a, b, (dims, ((), ())), preferred_element_type=F32)


def dot3(a, b, dims=((1,), (0,))):
    return dot(a[0], b[0], dims) + (dot(a[0], b[1], dims) + dot(a[1], b[0], dims))


def dot6(a, b, dims=((1,), (0,))):
    return lax.dot_general(a, b, (dims, ((), ())), precision=HIGHEST, preferred_element_type=F32)


class Links:
    def __init__(self, ssem, rsem):
        self.ssem, self.rsem = ssem, rsem
        self.r, self.c = lax.axis_index("row"), lax.axis_index("col")
        self.x, self.z = self.r // NZ, self.r % NZ

        x, z, c = self.x, self.z, self.c
        self.sign = 1 - 2 * lax.rem(c, 2)
        self.xs = {d: {"row": self.to_x(d) * NZ + z, "col": c} for d in (1, 2, 3)}
        self.zs = {d: {"row": x * NZ + self.to_z(d), "col": c} for d in (1, 4, 8, 12, 15)}
        self.qs = {d: {"row": x * NZ + (z // 4) * 4 + lax.rem(z + d, 4), "col": c} for d in (1, 2, 3)}
        self.cs = {d: {"row": self.r, "col": lax.rem(c + d, NC)} for d in range(1, NC)}

    def to_x(self, d):
        return lax.rem(self.x + self.sign * d + NX, NX)

    def to_z(self, d):
        return lax.rem(self.z + self.sign * d + NZ, NZ)

    def copy(self, src, dst, recv, device, slot=0):
        return pltpu.make_async_remote_copy(
            src_ref=src, dst_ref=dst, send_sem=self.ssem.at[slot], recv_sem=recv,
            device_id=device, device_id_type=pl.DeviceIdType.MESH)

    def send(self, src, dst, recv, device, slot):
        self.copy(src, dst, recv, device, slot).start()

    def recv(self, dst, sem):
        self.copy(dst, dst, sem, self.xs[1]).wait_recv()

    def sent(self, ref, slot):
        self.copy(ref, ref, self.rsem, self.xs[1], slot).wait_send()

    def greet(self, peers):
        barrier = pltpu.get_barrier_semaphore()
        for peer in peers:
            pl.semaphore_signal(barrier, inc=1, device_id=peer, device_id_type=pl.DeviceIdType.MESH)
        return lambda: pl.semaphore_wait(barrier, len(peers))


def block(b):
    return pl.ds(pl.multiple_of(b * BLK, BLK), BLK)


def split_rows(ref, b):
    parts = [split(ref[pl.ds(2 * BLK * b + h, BLK, stride=2), :]) for h in (0, 1)]
    return tuple(jnp.concatenate(p, axis=1) for p in zip(*parts))


def gather(t, buf, natural, sems, work, before_b=lambda: None):
    agaz, agax, agbx, agbz = sems
    xs, send, recv = t.xs, t.send, t.recv
    right, left = t.zs[1], t.zs[15]
    half = CA // 2

    def one(k):
        return buf.at[0, k, pl.ds(0, CA)]

    def two(i, k, n, lo=0, size=CA):
        return buf.at[i, pl.ds(k, n), pl.ds(lo, size)]

    def group(g, k):
        return buf.at[pl.ds(2 * g, 2), k, pl.ds(CA, CB)]

    def side(k, n, s):
        send(two(0, k, n), two(1, k, n), agax.at[0, s], xs[1], 0)
        send(two(0, k, n), two(3, k, n), agax.at[1, s], xs[3], 0)

    def forward(k, n, s):
        recv(two(1, k, n), agax.at[0, s])
        send(two(1, k, n, 0, half), two(2, k, n, 0, half), agax.at[2, s], xs[1], 0)
        recv(two(3, k, n), agax.at[1, s])
        send(two(3, k, n, half, half), two(2, k, n, half, half), agax.at[3, s], xs[3], 0)

    def finish(k, n, s):
        recv(two(2, k, n, 0, half), agax.at[2, s])
        recv(two(2, k, n, half, half), agax.at[3, s])

    send(one(0), one(1), agaz.at[0, 1], right, 0)
    send(one(0), one(2), agaz.at[1, 1], left, 0)
    before_b()
    for d in (1, 2, 3):
        send(buf.at[0, 0, pl.ds(CA, CB)], buf.at[d, 0, pl.ds(CA, CB)], agbx.at[d], xs[d], 0)
    side(0, 1, 0)
    for d in (1, 2, 3):
        recv(buf.at[d, 0, pl.ds(CA, CB)], agbx.at[d])
    for g in (0, 1):
        send(group(g, 0), group(g, 1), agbz.at[0, g, 1], right, 0)
        send(group(g, 0), group(g, 2), agbz.at[1, g, 1], left, 0)
    forward(0, 1, 0)

    def step(s, carry):
        kr, kl = 2 * s - 1, 2 * s
        recv(one(kr), agaz.at[0, s])
        send(one(kr), one(kr + 2), agaz.at[0, s + 1], right, 0)
        recv(one(kl), agaz.at[1, s])

        @pl.when(s < 7)
        def _():
            send(one(kl), one(kl + 2), agaz.at[1, s + 1], left, 0)

        side(kr, 2, s)
        for g in (0, 1):
            recv(group(g, kl), agbz.at[1, g, s])
            send(group(g, kl), group(g, jnp.minimum(kl + 2, 15)), agbz.at[1, g, s + 1], left, 0)
            recv(group(g, kr), agbz.at[0, g, s])

            @pl.when(s < 7)
            def _():
                send(group(g, kr), group(g, kr + 2), agbz.at[0, g, s + 1], right, 0)

        @pl.when(s > 1)
        def _():
            forward(kr - 2, 2, s - 1)

        work(s)
        return carry

    lax.fori_loop(1, 8, step, 0)
    recv(one(15), agaz.at[0, 8])
    side(15, 1, 8)
    forward(13, 2, 7)
    for g in (0, 1):
        recv(group(g, 15), agbz.at[1, g, 8])
    forward(15, 1, 8)
    finish(0, 1, 0)

    def last(s, carry):
        finish(2 * s - 1, 2, s)
        return carry

    lax.fori_loop(1, 8, last, 0)
    finish(15, 1, 8)
    t.sent(buf.reshape(NX * NZ * CH, 128).at[pl.ds(0, 6552)], 0)

    def place(s, carry):
        k = jnp.where(s == 0, 0, jnp.where(s > 8, 2 * (NZ - s), 2 * s - 1))
        n = t.to_z(-s)
        for i in range(NX):
            row = t.to_x(-i) * NZ + n
            natural[pl.ds(pl.multiple_of(CH * row, 8), CH), :] = buf[i, k]
        return carry

    lax.fori_loop(0, NZ, place, 0)


def factor_kernel(mom, grad, fac, rfh, rfl, basis, update, ownf,
                  momv, gradv, bhi, blo, thi, tlo, gat, gat2, ppart, precv, panel,
                  term, part, red, red2, xh, xf, za, zb, xb, gram, g0, g1, g2, g3, g4, aw, rfhv, rflv, sq, sqr,
                  lsem, ssem, tsem, agaz, agax, agbx, agbz, bgaz, bgax, bgbx, bgbz, psem,
                  rsx, rsza, rszb, rsxb, gsem, qsem, osem, *, n_cols, scale):
    t = Links(ssem, agbx.at[0])
    t2 = Links(tsem, agbx.at[0])
    r, c, x, z = t.r, t.c, t.x, t.z
    xs, zs, qs, cs, send, recv, sent = t.xs, t.zs, t.qs, t.cs, t.send, t.recv, t.sent
    loads = (pltpu.make_async_copy(mom, momv, lsem.at[0]), pltpu.make_async_copy(grad, gradv, lsem.at[1]))
    for load in loads:
        load.start()
    greeted = t.greet([*xs.values(), *zs.values(), *qs.values(), *cs.values()])

    gat.at[0, 0][pl.ds(0, CH // 2, stride=2), :] = fac[:, :128]
    gat.at[0, 0][pl.ds(1, CH // 2, stride=2), :] = fac[:, 128:]
    greeted()

    def prepare(b):
        at = block(b)
        value = momv[:, at] + gradv[:, at].astype(F32)
        high, low = split(value)
        bhi[:, at], blo[:, at] = high, low
        high, low = split(value.T)
        thi[at, :], tlo[at, :] = high, low

    def prepare_step(s):
        @pl.when(s == 1)
        def _():
            for load in loads:
                load.wait()

        prepare(2 * s - 2)

        @pl.when(s < 7)
        def _():
            prepare(2 * s - 1)

    gather(t, gat, gat2, (agaz, agax, agbx, agbz), prepare_step)

    def panel_step(b, total):
        at = block(b)
        return total + dot3((bhi[:, at], blo[:, at]), split_rows(gat2, b))

    total = lax.fori_loop(0, NBLK, panel_step, jnp.zeros((ROWS, RANK), F32))
    ppart[...] = total.reshape(NC, ROWS // NC, RANK)
    for d in range(1, NC):
        send(ppart.at[cs[d]["col"]], precv.at[d], psem.at[0, d], cs[d], 1)
    mine = ppart[c]
    for d in range(1, NC):
        recv(precv.at[d], psem.at[0, d])
        mine = mine + precv[d]
    panel[c] = mine
    for d in range(1, NC):
        send(panel.at[c], panel.at[c], psem.at[1, d], cs[d], 1)
    for d in range(1, NC):
        recv(panel.at[lax.rem(c - d + NC, NC)], psem.at[1, d])
    sent(gat2.at[pl.ds(0, 14 * 32)], 1)

    left = panel[...].reshape(ROWS, RANK)
    gram[...] = dot6(left.T, left)

    def gram_rows(xi):
        return pl.ds(pl.multiple_of(32 * c + 8 * xi, 8), 8)

    for d in (1, 2, 3):
        send(gram.at[gram_rows(t.to_x(d))], g0.at[d], gsem.at[0, d], xs[d], 2)

    def gram_0():
        total = gram[gram_rows(x), :]
        for d in (1, 2, 3):
            recv(g0.at[d], gsem.at[0, d])
            total = total + g0[d]
        g1[0] = total
        for d in (1, 2, 3):
            send(g1.at[0], g1.at[d], gsem.at[1, d], qs[d], 2)

    def gram_1():
        total = g1[0]
        for d in (1, 2, 3):
            recv(g1.at[d], gsem.at[1, d])
            total = total + g1[d]
        g2[0] = total
        for d in (1, 2, 3):
            send(g2.at[0], g2.at[d], gsem.at[2, d], zs[4 * d], 2)

    def gram_2():
        total = g2[0]
        for d in (1, 2, 3):
            recv(g2.at[d], gsem.at[2, d])
            total = total + g2[d]
        g3[x] = total
        for d in (1, 2, 3):
            send(g3.at[x], g3.at[x], gsem.at[3, d], xs[d], 2)

    def gram_3():
        for d in (1, 2, 3):
            recv(g3.at[t.to_x(-d)], gsem.at[3, d])
        g4[c] = g3[...]
        for d in range(1, NC):
            send(g4.at[c], g4.at[c], gsem.at[4, d], cs[d], 3)

    def gram_4():
        for d in range(1, NC):
            recv(g4.at[lax.rem(c - d + NC, NC)], gsem.at[4, d])
        aw[...] = g4[...].reshape(RANK, RANK)
        sent(gram.at[pl.ds(0, 96)], 2)
        sent(g4.at[pl.ds(0, NC - 1)], 3)

    sub = lax.broadcasted_iota(jnp.int32, (NB, 128), 0)
    lane = lax.broadcasted_iota(jnp.int32, (NB, 128), 1)
    sub_w = lax.broadcasted_iota(jnp.int32, (NB, RANK), 0)
    lane_w = lax.broadcasted_iota(jnp.int32, (NB, RANK), 1)
    i_all = lax.broadcasted_iota(jnp.int32, (RANK, RANK), 0)
    j_all = lax.broadcasted_iota(jnp.int32, (RANK, RANK), 1)

    def factor_block(k):
        first = pl.multiple_of(NB * k, NB)
        rows = aw[pl.ds(first, NB), :]
        near = jnp.where(k < 4, rows[:, :128], rows[:, 128:])
        near = pltpu.roll(near, lax.rem(128 - NB * lax.rem(k, 4), 128), 1)
        e = jnp.where(lane < NB, near, jnp.where(lane - NB == sub, 1.0, 0.0))
        for j in range(0, NB, 4):
            cols = [jnp.broadcast_to(e[:, j + i:j + i + 1], (NB, 128)) for i in range(4)]
            pivots = [e[j + i:j + i + 1, :] for i in range(4)]
            for i in range(4):
                at = slice(j + i, j + i + 1)
                ratio = jnp.where(sub > j + i, cols[i] * (1.0 / cols[i][at, :]), 0.0)
                for m in range(i + 1, 4):
                    cols[m] = cols[m] - ratio * cols[m][at, :]
                    pivots[m] = pivots[m] - ratio[j + m:j + m + 1, :] * pivots[i]
                e = e - ratio * pivots[i]
        diagonal = jnp.sum(jnp.where(lane == sub, e, 0.0), axis=1, keepdims=True)
        inverse = (e * (1.0 / jnp.sqrt(diagonal)))[:, NB:2 * NB]
        here = (lane_w >= first) & (lane_w < first + NB)
        rows = jnp.where(here, jnp.where(lane_w - first == sub_w, 1.0, 0.0), rows)
        rows = dot6(inverse, rows)
        below = jnp.where(lane_w >= first + NB, rows, 0.0)
        done = (i_all >= first + NB) & (j_all >= first) & (j_all < first + NB)
        aw[...] = jnp.where(done, 0.0, aw[...]) - dot6(below.T, rows)
        aw[pl.ds(first, NB), :] = rows

    lp = split(left)

    def term_step(b, carry):
        h = dot3((thi[block(b), :], tlo[block(b), :]), lp)
        term[pl.ds(2 * BLK * b, BLK, stride=2), :] = h[:, :128]
        term[pl.ds(2 * BLK * b + 1, BLK, stride=2), :] = h[:, 128:]
        pl.when(b == 6)(gram_0)
        return carry

    lax.fori_loop(0, NBLK, term_step, 0)
    gram_1()

    def place(k, carry):
        n = t.to_z(jnp.where(k == 15, 0, jnp.where(lax.rem(k, 2) == 0, 8 - k // 2, k // 2 - 7)))
        for i in range(NX):
            row = t.to_x(i) * NZ + n
            part[i, k] = term[pl.ds(pl.multiple_of(CH * row, 8), CH), :]
        return carry

    lax.fori_loop(0, NZ, place, 0)

    half = CA // 2

    def pair(i, s, lo=0, size=CA):
        return part.at[i, pl.ds(2 * s, 2), pl.ds(lo, size)]

    def send_half(s):
        send(pair(2, s, 0, half), xh.at[0, s], rsx.at[0, s], xs[1], 4)
        send(pair(2, s, half, half), xh.at[1, s], rsx.at[1, s], xs[3], 4)

    def send_full(s):
        two = pl.ds(2 * s, 2)
        recv(xh.at[0, s], rsx.at[0, s])
        part[1, two, :half, :] += xh[0, s]
        send(pair(1, s), xf.at[0, s], rsx.at[2, s], xs[1], 4)
        recv(xh.at[1, s], rsx.at[1, s])
        part[3, two, half:CA, :] += xh[1, s]
        send(pair(3, s), xf.at[1, s], rsx.at[3, s], xs[3], 4)

    def take_full(s):
        two = pl.ds(2 * s, 2)
        recv(xf.at[0, s], rsx.at[2, s])
        recv(xf.at[1, s], rsx.at[3, s])
        part[0, two, :CA, :] += xf[0, s] + xf[1, s]

    send_half(0)
    send_half(1)
    send_full(0)

    def reduce_step(s, carry):
        @pl.when(s < 6)
        def _():
            send_half(s + 2)

        for i, g in enumerate((1, 0)):
            rows = pl.ds(2 * g, 2)
            kl, kr = jnp.maximum(2 * s - 1, 0), 2 * s + 2

            @pl.when(s > 0)
            def _():
                recv(zb.at[1, i, s], rszb.at[1, i, s])
                part[rows, kl, CA:, :] += zb[1, i, s]

            send(part.at[rows, kl, pl.ds(CA, CB)], zb.at[1, i, s + 1], rszb.at[1, i, s + 1], zs[15], 4)

            @pl.when(s < 7)
            def _():
                @pl.when(s > 0)
                def _():
                    recv(zb.at[0, i, s], rszb.at[0, i, s])
                    part[rows, kr, CA:, :] += zb[0, i, s]

                send(part.at[rows, kr, pl.ds(CA, CB)], zb.at[0, i, s + 1], rszb.at[0, i, s + 1], zs[1], 4)

        @pl.when(s < 7)
        def _():
            send_full(s + 1)

        take_full(s)

        @pl.when(s > 0)
        def _():
            recv(za.at[0, s], rsza.at[0, s])
            part[0, 2 * s, :CA, :] += za[0, s]

        send(part.at[0, 2 * s, pl.ds(0, CA)], za.at[0, s + 1], rsza.at[0, s + 1], zs[1], 4)

        @pl.when(s < 7)
        def _():
            @pl.when(s > 0)
            def _():
                recv(za.at[1, s], rsza.at[1, s])
                part[0, 2 * s + 1, :CA, :] += za[1, s]

            send(part.at[0, 2 * s + 1, pl.ds(0, CA)], za.at[1, s + 1], rsza.at[1, s + 1], zs[15], 4)

        for when, stage in enumerate((gram_2, gram_3, gram_4)):
            pl.when(s == when)(stage)

        @pl.when(s > 2)
        def _():
            factor_block(s - 3)

        return carry

    lax.fori_loop(0, 8, reduce_step, 0)
    for i, g in enumerate((1, 0)):
        recv(zb.at[1, i, 8], rszb.at[1, i, 8])
        recv(zb.at[0, i, 7], rszb.at[0, i, 7])
        part[2 * g:2 * g + 2, 15, CA:, :] += zb[1, i, 8] + zb[0, i, 7]
    for d in (1, 2, 3):
        send(part.at[d, 15, pl.ds(CA, CB)], xb.at[d], rsxb.at[d], xs[d], 4)
    recv(za.at[0, 8], rsza.at[0, 8])
    recv(za.at[1, 7], rsza.at[1, 7])
    red[0, 0, :CA, :] = part[0, 15, :CA, :] + (za[0, 8] + za[1, 7])

    def finish_b():
        total = part[0, 15, CA:, :]
        for d in (1, 2, 3):
            recv(xb.at[d], rsxb.at[d])
            total = total + xb[d]
        red[0, 0, CA:, :] = total

    def factor_rest(s):
        @pl.when(s < 4)
        def _():
            factor_block(s + 4)

    gather(t2, red, red2, (bgaz, bgax, bgbx, bgbz), factor_rest, finish_b)
    sent(term.at[pl.ds(0, 6552)], 4)

    inverse = jnp.where(i_all >= j_all, aw[...], 0.0)
    nt = ((1,), (1,))
    inv = split(inverse)

    def right_step(b, squares):
        rf = dot3(split_rows(red2, b), inv, nt)
        rfhv[block(b), :], rflv[block(b), :] = split(rf)
        return squares + jnp.sum((rf * rf).reshape(BLK // 8, 8, RANK), axis=0)

    squares = lax.fori_loop(0, NBLK, right_step, jnp.zeros((8, RANK), F32))
    stores = (pltpu.make_async_copy(rfhv, rfh, osem.at[0]), pltpu.make_async_copy(rflv, rfl, osem.at[1]))
    for store in stores:
        store.start()
    sq[...] = squares
    for d in range(1, NC):
        send(sq, sqr.at[d], qsem.at[d], cs[d], 6)
    left_basis = dot6(left, inverse, nt)
    halves = [red.at[0, 0][pl.ds(h, CH // 2, stride=2), :] for h in (0, 1)]
    own_rf = dot6(jnp.concatenate(halves, axis=1), inverse, nt)
    for d in range(1, NC):
        recv(sqr.at[d], qsem.at[d])
        squares = squares + sqr[d]
    rms = jnp.sqrt(jnp.sum(squares, axis=0, keepdims=True) * (1.0 / n_cols) + EPSILON)
    ownf[...] = own_rf / rms
    basis[...] = left_basis * -(1.0 - MOMENTUM_KEEP)
    update[...] = left_basis * (-scale / rms)
    sent(gram.at[pl.ds(0, 8 * (NC - 1))], 6)
    for store in stores:
        store.wait()


def output_kernel(mom, grad, rfh, rfl, basis, update, ownf, momo, wupd, faco):
    nt = ((1,), (1,))
    high, low = split(update[...])
    rows = jnp.concatenate([basis[...].astype(BF16), high, low], axis=0)
    for first in range(0, HALF, BLK):
        at = slice(first, min(first + BLK, HALF))
        product = dot(rows, rfh[at, :], nt)
        momo[:, at] = mom[:, at] + grad[:, at].astype(F32) + product[:ROWS]
        wupd[:, at] = (product[ROWS:2 * ROWS] + (product[2 * ROWS:] + dot(high, rfl[at, :], nt))).astype(BF16)

    @pl.when(pl.program_id(0) == 0)
    def _():
        faco[...] = ownf[...]


def shards(momentum, gradient, factor):
    rows = momentum.shape[0] * lax.axis_size("row")
    n_cols = momentum.shape[1] * lax.axis_size("col")
    scale = STEP_SIZE * math.sqrt(rows / factor.shape[1])
    dma, vmem, hbm = pltpu.SemaphoreType.DMA, pltpu.VMEM, pl.BlockSpec(memory_space=pl.ANY)
    inside = pl.BlockSpec(memory_space=pltpu.VMEM)
    shape = jax.ShapeDtypeStruct
    flat, natural = vmem((NX, NZ, CH, 128), F32), vmem((NX * NZ * CH, 128), F32)
    gather_sems = [dma((2, 9)), dma((4, 9)), dma((4,)), dma((2, 2, 9))]
    rows16 = vmem((NC, ROWS // NC, RANK), F32)
    small = vmem((4, 8, RANK), F32)
    wide, tall, full = vmem((ROWS, COLS), BF16), vmem((COLS, ROWS), BF16), vmem((COLS, RANK), BF16)
    rfh, rfl, basis, update, ownf = pl.pallas_call(
        functools.partial(factor_kernel, n_cols=n_cols, scale=scale),
        out_shape=(
            shape((COLS, RANK), BF16), shape((COLS, RANK), BF16),
            shape((ROWS, RANK), F32), shape((ROWS, RANK), F32), shape((CH // 2, RANK), F32)),
        in_specs=[hbm, hbm, inside],
        out_specs=(hbm, hbm, inside, inside, inside),
        scratch_shapes=[
            vmem((ROWS, COLS), F32), wide, wide, wide, tall, tall, flat, natural, rows16, rows16, rows16,
            natural, flat, flat, natural, vmem((2, 8, 2, CA // 2, 128), F32), vmem((2, 8, 2, CA, 128), F32),
            vmem((2, 9, CA, 128), F32), vmem((2, 2, 9, 2, CB, 128), F32), vmem((4, CB, 128), F32),
            vmem((RANK, RANK), F32), small, small, small, small, vmem((NC, 4, 8, RANK), F32),
            vmem((RANK, RANK), F32), full, full, vmem((8, RANK), F32), vmem((NC, 8, RANK), F32),
            dma((2,)), dma((7,)), dma((1,)), *gather_sems, *gather_sems, dma((2, NC)),
            dma((4, 8)), dma((2, 9)), dma((2, 2, 9)), dma((4,)), dma((5, NC)), dma((NC,)), dma((2,)),
        ],
        compiler_params=pltpu.CompilerParams(collective_id=0, has_side_effects=True, vmem_limit_bytes=60 * 2**20),
        name="right_factor",
    )(momentum, gradient, factor)
    whole = pl.BlockSpec((ROWS, RANK), lambda b: (0, 0))
    across = pl.BlockSpec((ROWS, HALF), lambda b: (0, b))
    down = pl.BlockSpec((HALF, RANK), lambda b: (b, 0))
    chunk = pl.BlockSpec((CH // 2, RANK), lambda b: (0, 0))
    return pl.pallas_call(
        output_kernel,
        grid=(2,),
        out_shape=(shape((ROWS, COLS), F32), shape((ROWS, COLS), BF16), shape((CH // 2, RANK), F32)),
        in_specs=[across, across, down, down, whole, whole, chunk],
        out_specs=(across, across, chunk),
        compiler_params=pltpu.CompilerParams(vmem_limit_bytes=60 * 2**20),
        name="outputs",
    )(momentum, gradient, rfh, rfl, basis, update, ownf)


def solution(mesh):
    placed = (P("row", "col"), P("row", "col"), P(("col", "row"), None))
    return jax.shard_map(shards, mesh=mesh, in_specs=placed, out_specs=placed, check_vma=False)
```

```python
import functools
import math

import jax
import jax.numpy as jnp
from jax import lax
from jax.experimental import pallas as pl
from jax.experimental.pallas import tpu as pltpu
from jax.sharding import PartitionSpec as P

HIGHEST = lax.Precision.HIGHEST
MOMENTUM_KEEP = 0.8
STEP_SIZE = 0.3
EPSILON = 1e-06
F32 = jnp.float32
BF16 = jnp.bfloat16

NX, NZ = 4, 16
NC = 8
CH = 104
CA = 80
CB = CH - CA
ROWS, COLS, RANK = 128, 3328, 256
BLK = 256
NBLK = COLS // BLK
HALF = COLS // 2
NB = 32


def split(value):
    high = value.astype(BF16)
    return high, (value - high.astype(F32)).astype(BF16)


def dot(a, b, dims=((1,), (0,))):
    return lax.dot_general(a, b, (dims, ((), ())), preferred_element_type=F32)


def dot3(a, b, dims=((1,), (0,))):
    return dot(a[0], b[0], dims) + (dot(a[0], b[1], dims) + dot(a[1], b[0], dims))


def dot6(a, b, dims=((1,), (0,))):
    return lax.dot_general(a, b, (dims, ((), ())), precision=HIGHEST, preferred_element_type=F32)


class Links:
    def __init__(self, ssem, rsem):
        self.ssem, self.rsem = ssem, rsem
        self.r, self.c = lax.axis_index("row"), lax.axis_index("col")
        self.x, self.z = self.r // NZ, self.r % NZ

        x, z, c = self.x, self.z, self.c
        self.sign = 1 - 2 * lax.rem(c, 2)
        self.xs = {d: {"row": self.to_x(d) * NZ + z, "col": c} for d in (1, 2, 3)}
        self.zs = {d: {"row": x * NZ + self.to_z(d), "col": c} for d in (1, 4, 5, 8, 11, 12, 15)}
        self.qs = {d: {"row": x * NZ + (z // 4) * 4 + lax.rem(z + d, 4), "col": c} for d in (1, 2, 3)}
        self.cs = {d: {"row": self.r, "col": lax.rem(c + d, NC)} for d in range(1, NC)}

    def to_x(self, d):
        return lax.rem(self.x + self.sign * d + NX, NX)

    def to_z(self, d):
        return lax.rem(self.z + self.sign * d + NZ, NZ)

    def copy(self, src, dst, recv, device, slot=0):
        return pltpu.make_async_remote_copy(
            src_ref=src, dst_ref=dst, send_sem=self.ssem.at[slot], recv_sem=recv,
            device_id=device, device_id_type=pl.DeviceIdType.MESH)

    def send(self, src, dst, recv, device, slot):
        self.copy(src, dst, recv, device, slot).start()

    def recv(self, dst, sem):
        self.copy(dst, dst, sem, self.xs[1]).wait_recv()

    def sent(self, ref, slot):
        self.copy(ref, ref, self.rsem, self.xs[1], slot).wait_send()

    def greet(self, peers):
        barrier = pltpu.get_barrier_semaphore()
        for peer in peers:
            pl.semaphore_signal(barrier, inc=1, device_id=peer, device_id_type=pl.DeviceIdType.MESH)
        return lambda: pl.semaphore_wait(barrier, len(peers))


def block(b):
    return pl.ds(pl.multiple_of(b * BLK, BLK), BLK)


def split_rows(ref, b):
    parts = [split(ref[pl.ds(2 * BLK * b + h, BLK, stride=2), :]) for h in (0, 1)]
    return tuple(jnp.concatenate(p, axis=1) for p in zip(*parts))


SLOT = {0: 0, 1: 1, 15: 2, 5: 3, 11: 4, 2: 5, 14: 6, 6: 7, 10: 8, 4: 9, 12: 10, 7: 11, 9: 12, 3: 13, 13: 14, 8: 15}
GROUPS = ((0, 1), (1, 2), (3, 2), (5, 2), (7, 4), (11, 4), (15, 1))


def gather(t, buf, natural, sems, work, before_b=lambda: None):
    zsem, xsem, bsem, bxsem = sems
    xs, send, recv = t.xs, t.send, t.recv
    right, left, far_right, far_left = t.zs[1], t.zs[15], t.zs[5], t.zs[11]
    half = CA // 2

    def one(k, lo=0, size=CA):
        return buf.at[0, k, pl.ds(lo, size)]

    def four(k):
        return buf.at[pl.ds(0, NX), k, pl.ds(CA, CB)]

    def many(i, g, lo=0, size=CA):
        return buf.at[i, pl.ds(GROUPS[g][0], GROUPS[g][1]), pl.ds(lo, size)]

    def pass_a(k, *ways):
        if k:
            recv(one(k), zsem.at[k])
        for to, device in ways:
            send(one(k), one(to), zsem.at[to], device, 0)

    def pass_b(k, *ways):
        if k:
            recv(four(k), bsem.at[k])
        for to, device in ways:
            send(four(k), four(to), bsem.at[to], device, 0)

    def side(g):
        send(many(0, g), many(1, g), xsem.at[0, g], xs[1], 0)
        send(many(0, g), many(3, g), xsem.at[1, g], xs[3], 0)

    def forward(g):
        recv(many(1, g), xsem.at[0, g])
        send(many(1, g, 0, half), many(2, g, 0, half), xsem.at[2, g], xs[1], 0)
        recv(many(3, g), xsem.at[1, g])
        send(many(3, g, half, half), many(2, g, half, half), xsem.at[3, g], xs[3], 0)

    pass_a(0, (3, far_right), (4, far_left), (1, right), (2, left))
    before_b()
    for d in (1, 2, 3):
        send(buf.at[0, 0, pl.ds(CA, CB)], buf.at[d, 0, pl.ds(CA, CB)], bxsem.at[d], xs[d], 0)
    side(0)
    for d in (1, 2, 3):
        recv(buf.at[d, 0, pl.ds(CA, CB)], bxsem.at[d])
    pass_b(0, (3, far_right), (4, far_left), (1, right), (2, left))
    work(0)
    pass_a(1, (5, right))
    pass_a(2, (6, left))
    side(1)
    forward(0)
    pass_a(3, (7, right), (9, left))
    pass_a(4, (8, left), (10, right))
    side(2)
    pass_b(1, (5, right))
    pass_b(2, (6, left))
    work(1)
    pass_b(3, (7, right), (9, left))
    pass_b(4, (8, left), (10, right))
    forward(1)
    pass_a(5)
    pass_a(6)
    side(3)
    pass_a(7, (11, right))
    pass_a(8, (12, left))
    pass_a(9, (13, left))
    pass_a(10, (14, right))
    side(4)
    forward(2)
    pass_b(5)
    pass_b(6)
    pass_b(7, (11, right))
    pass_b(8, (12, left))
    pass_b(9, (13, left))
    pass_b(10, (14, right))
    work(2)
    forward(3)
    pass_a(11)
    pass_a(12)
    send(one(11, 0, half), one(15, 0, half), zsem.at[15], right, 0)
    send(one(12, half, half), one(15, half, half), zsem.at[16], left, 0)
    pass_a(13)
    pass_a(14)
    side(5)
    pass_b(11)
    pass_b(12, (15, left))
    forward(4)
    recv(one(15, 0, half), zsem.at[15])
    recv(one(15, half, half), zsem.at[16])
    side(6)
    pass_b(13)
    pass_b(14)
    work(3)
    forward(5)
    forward(6)
    pass_b(15)
    for g in range(len(GROUPS)):
        recv(many(2, g, 0, half), xsem.at[2, g])
        recv(many(2, g, half, half), xsem.at[3, g])
    t.sent(natural.at[pl.ds(0, 6552)], 0)

    for d, k in SLOT.items():
        n = t.to_z(-d)
        for i in range(NX):
            row = t.to_x(-i) * NZ + n
            natural[pl.ds(pl.multiple_of(CH * row, 8), CH), :] = buf[i, k]


def factor_kernel(mom, grad, fac, rfh, rfl, basis, update, ownf,
                  momv, gradv, bhi, blo, thi, tlo, gat, gat2, ppart, precv, panel,
                  term, part, red, red2, xh, xf, za, zb, xb, gram, g0, g1, g2, g3, g4, aw, rfhv, rflv, sq, sqr,
                  lsem, ssem, tsem, agaz, agax, agbz, agbx, bgaz, bgax, bgbz, bgbx, psem,
                  rsx, rsza, rszb, rsxb, gsem, qsem, osem, *, n_cols, scale):
    t = Links(ssem, psem.at[0, 0])
    t2 = Links(tsem, psem.at[0, 0])
    r, c, x, z = t.r, t.c, t.x, t.z
    xs, zs, qs, cs, send, recv, sent = t.xs, t.zs, t.qs, t.cs, t.send, t.recv, t.sent
    loads = (pltpu.make_async_copy(mom, momv, lsem.at[0]), pltpu.make_async_copy(grad, gradv, lsem.at[1]))
    for load in loads:
        load.start()
    greeted = t.greet([*xs.values(), *zs.values(), *qs.values(), *cs.values()])

    gat.at[0, 0][pl.ds(0, CH // 2, stride=2), :] = fac[:, :128]
    gat.at[0, 0][pl.ds(1, CH // 2, stride=2), :] = fac[:, 128:]
    greeted()

    def prepare(b):
        at = block(b)
        value = momv[:, at] + gradv[:, at].astype(F32)
        high, low = split(value)
        bhi[:, at], blo[:, at] = high, low
        high, low = split(value.T)
        thi[at, :], tlo[at, :] = high, low

    def prepare_some(i):
        if i == 0:
            for load in loads:
                load.wait()

        def step(b, carry):
            prepare(b)
            return carry

        lax.fori_loop(*((0, 3), (3, 6), (6, 10), (10, NBLK))[i], step, 0)

    gather(t, gat, gat2, (agaz, agax, agbz, agbx), prepare_some)

    def panel_step(b, total):
        at = block(b)
        return total + dot3((bhi[:, at], blo[:, at]), split_rows(gat2, b))

    total = lax.fori_loop(0, NBLK, panel_step, jnp.zeros((ROWS, RANK), F32))
    ppart[...] = total.reshape(NC, ROWS // NC, RANK)
    for d in range(1, NC):
        send(ppart.at[cs[d]["col"]], precv.at[d], psem.at[0, d], cs[d], 1)
    mine = ppart[c]
    for d in range(1, NC):
        recv(precv.at[d], psem.at[0, d])
        mine = mine + precv[d]
    panel[c] = mine
    for d in range(1, NC):
        send(panel.at[c], panel.at[c], psem.at[1, d], cs[d], 1)
    for d in range(1, NC):
        recv(panel.at[lax.rem(c - d + NC, NC)], psem.at[1, d])
    sent(gat2.at[pl.ds(0, 14 * 32)], 1)

    left = panel[...].reshape(ROWS, RANK)
    gram[...] = dot6(left.T, left)

    def gram_rows(xi):
        return pl.ds(pl.multiple_of(32 * c + 8 * xi, 8), 8)

    for d in (1, 2, 3):
        send(gram.at[gram_rows(t.to_x(d))], g0.at[d], gsem.at[0, d], xs[d], 2)

    def gram_0():
        total = gram[gram_rows(x), :]
        for d in (1, 2, 3):
            recv(g0.at[d], gsem.at[0, d])
            total = total + g0[d]
        g1[0] = total
        for d in (1, 2, 3):
            send(g1.at[0], g1.at[d], gsem.at[1, d], qs[d], 2)

    def gram_1():
        total = g1[0]
        for d in (1, 2, 3):
            recv(g1.at[d], gsem.at[1, d])
            total = total + g1[d]
        g2[0] = total
        for d in (1, 2, 3):
            send(g2.at[0], g2.at[d], gsem.at[2, d], zs[4 * d], 2)

    def gram_2():
        total = g2[0]
        for d in (1, 2, 3):
            recv(g2.at[d], gsem.at[2, d])
            total = total + g2[d]
        g3[x] = total
        for d in (1, 2, 3):
            send(g3.at[x], g3.at[x], gsem.at[3, d], xs[d], 2)

    def gram_3():
        for d in (1, 2, 3):
            recv(g3.at[t.to_x(-d)], gsem.at[3, d])
        g4[c] = g3[...]
        for d in range(1, NC):
            send(g4.at[c], g4.at[c], gsem.at[4, d], cs[d], 3)

    def gram_4():
        for d in range(1, NC):
            recv(g4.at[lax.rem(c - d + NC, NC)], gsem.at[4, d])
        aw[...] = g4[...].reshape(RANK, RANK)
        sent(gram.at[pl.ds(0, 96)], 2)
        sent(g4.at[pl.ds(0, NC - 1)], 3)

    sub = lax.broadcasted_iota(jnp.int32, (NB, 128), 0)
    lane = lax.broadcasted_iota(jnp.int32, (NB, 128), 1)
    sub_w = lax.broadcasted_iota(jnp.int32, (NB, RANK), 0)
    lane_w = lax.broadcasted_iota(jnp.int32, (NB, RANK), 1)
    i_all = lax.broadcasted_iota(jnp.int32, (RANK, RANK), 0)
    j_all = lax.broadcasted_iota(jnp.int32, (RANK, RANK), 1)

    def factor_block(k):
        first = pl.multiple_of(NB * k, NB)
        rows = aw[pl.ds(first, NB), :]
        near = jnp.where(k < 4, rows[:, :128], rows[:, 128:])
        near = pltpu.roll(near, lax.rem(128 - NB * lax.rem(k, 4), 128), 1)
        e = jnp.where(lane < NB, near, jnp.where(lane - NB == sub, 1.0, 0.0))
        for j in range(0, NB, 4):
            cols = [jnp.broadcast_to(e[:, j + i:j + i + 1], (NB, 128)) for i in range(4)]
            pivots = [e[j + i:j + i + 1, :] for i in range(4)]
            for i in range(4):
                at = slice(j + i, j + i + 1)
                ratio = jnp.where(sub > j + i, cols[i] * (1.0 / cols[i][at, :]), 0.0)
                for m in range(i + 1, 4):
                    cols[m] = cols[m] - ratio * cols[m][at, :]
                    pivots[m] = pivots[m] - ratio[j + m:j + m + 1, :] * pivots[i]
                e = e - ratio * pivots[i]
        diagonal = jnp.sum(jnp.where(lane == sub, e, 0.0), axis=1, keepdims=True)
        inverse = (e * (1.0 / jnp.sqrt(diagonal)))[:, NB:2 * NB]
        here = (lane_w >= first) & (lane_w < first + NB)
        rows = jnp.where(here, jnp.where(lane_w - first == sub_w, 1.0, 0.0), rows)
        rows = dot6(inverse, rows)
        below = jnp.where(lane_w >= first + NB, rows, 0.0)
        done = (i_all >= first + NB) & (j_all >= first) & (j_all < first + NB)
        aw[...] = jnp.where(done, 0.0, aw[...]) - dot6(below.T, rows)
        aw[pl.ds(first, NB), :] = rows

    lp = split(left)

    def term_step(b, carry):
        h = dot3((thi[block(b), :], tlo[block(b), :]), lp)
        term[pl.ds(2 * BLK * b, BLK, stride=2), :] = h[:, :128]
        term[pl.ds(2 * BLK * b + 1, BLK, stride=2), :] = h[:, 128:]
        pl.when(b == 6)(gram_0)
        return carry

    lax.fori_loop(0, NBLK, term_step, 0)
    gram_1()

    def place(k, carry):
        n = t.to_z(jnp.where(k == 15, 0, jnp.where(lax.rem(k, 2) == 0, 8 - k // 2, k // 2 - 7)))
        for i in range(NX):
            row = t.to_x(i) * NZ + n
            part[i, k] = term[pl.ds(pl.multiple_of(CH * row, 8), CH), :]
        return carry

    lax.fori_loop(0, NZ, place, 0)

    half = CA // 2

    def pair(i, s, lo=0, size=CA):
        return part.at[i, pl.ds(2 * s, 2), pl.ds(lo, size)]

    def send_half(s):
        send(pair(2, s, 0, half), xh.at[0, s], rsx.at[0, s], xs[1], 4)
        send(pair(2, s, half, half), xh.at[1, s], rsx.at[1, s], xs[3], 4)

    def send_full(s):
        two = pl.ds(2 * s, 2)
        recv(xh.at[0, s], rsx.at[0, s])
        part[1, two, :half, :] += xh[0, s]
        send(pair(1, s), xf.at[0, s], rsx.at[2, s], xs[1], 4)
        recv(xh.at[1, s], rsx.at[1, s])
        part[3, two, half:CA, :] += xh[1, s]
        send(pair(3, s), xf.at[1, s], rsx.at[3, s], xs[3], 4)

    def take_full(s):
        two = pl.ds(2 * s, 2)
        recv(xf.at[0, s], rsx.at[2, s])
        recv(xf.at[1, s], rsx.at[3, s])
        part[0, two, :CA, :] += xf[0, s] + xf[1, s]

    send_half(0)
    send_half(1)
    send_full(0)

    def reduce_step(s, carry):
        @pl.when(s < 6)
        def _():
            send_half(s + 2)

        for i, g in enumerate((1, 0)):
            rows = pl.ds(2 * g, 2)
            kl, kr = jnp.maximum(2 * s - 1, 0), 2 * s + 2

            @pl.when(s > 0)
            def _():
                recv(zb.at[1, i, s], rszb.at[1, i, s])
                part[rows, kl, CA:, :] += zb[1, i, s]

            send(part.at[rows, kl, pl.ds(CA, CB)], zb.at[1, i, s + 1], rszb.at[1, i, s + 1], zs[15], 4)

            @pl.when(s < 7)
            def _():
                @pl.when(s > 0)
                def _():
                    recv(zb.at[0, i, s], rszb.at[0, i, s])
                    part[rows, kr, CA:, :] += zb[0, i, s]

                send(part.at[rows, kr, pl.ds(CA, CB)], zb.at[0, i, s + 1], rszb.at[0, i, s + 1], zs[1], 4)

        @pl.when(s < 7)
        def _():
            send_full(s + 1)

        take_full(s)

        @pl.when(s > 0)
        def _():
            recv(za.at[0, s], rsza.at[0, s])
            part[0, 2 * s, :CA, :] += za[0, s]

        send(part.at[0, 2 * s, pl.ds(0, CA)], za.at[0, s + 1], rsza.at[0, s + 1], zs[1], 4)

        @pl.when(s < 7)
        def _():
            @pl.when(s > 0)
            def _():
                recv(za.at[1, s], rsza.at[1, s])
                part[0, 2 * s + 1, :CA, :] += za[1, s]

            send(part.at[0, 2 * s + 1, pl.ds(0, CA)], za.at[1, s + 1], rsza.at[1, s + 1], zs[15], 4)

        for when, stage in enumerate((gram_2, gram_3, gram_4)):
            pl.when(s == when)(stage)

        @pl.when(s > 2)
        def _():
            factor_block(s - 3)

        return carry

    lax.fori_loop(0, 8, reduce_step, 0)
    for i, g in enumerate((1, 0)):
        recv(zb.at[1, i, 8], rszb.at[1, i, 8])
        recv(zb.at[0, i, 7], rszb.at[0, i, 7])
        part[2 * g:2 * g + 2, 15, CA:, :] += zb[1, i, 8] + zb[0, i, 7]
    for d in (1, 2, 3):
        send(part.at[d, 15, pl.ds(CA, CB)], xb.at[d], rsxb.at[d], xs[d], 4)
    recv(za.at[0, 8], rsza.at[0, 8])
    recv(za.at[1, 7], rsza.at[1, 7])
    red[0, 0, :CA, :] = part[0, 15, :CA, :] + (za[0, 8] + za[1, 7])

    def finish_b():
        total = part[0, 15, CA:, :]
        for d in (1, 2, 3):
            recv(xb.at[d], rsxb.at[d])
            total = total + xb[d]
        red[0, 0, CA:, :] = total

    def factor_rest(i):
        if i:
            factor_block(jnp.int32(i + 4))

    gather(t2, red, red2, (bgaz, bgax, bgbz, bgbx), factor_rest, finish_b)
    sent(term.at[pl.ds(0, 6552)], 4)

    inverse = jnp.where(i_all >= j_all, aw[...], 0.0)
    nt = ((1,), (1,))
    inv = split(inverse)

    def right_step(b, squares):
        rf = dot3(split_rows(red2, b), inv, nt)
        rfhv[block(b), :], rflv[block(b), :] = split(rf)
        return squares + jnp.sum((rf * rf).reshape(BLK // 8, 8, RANK), axis=0)

    squares = lax.fori_loop(0, NBLK, right_step, jnp.zeros((8, RANK), F32))
    stores = (pltpu.make_async_copy(rfhv, rfh, osem.at[0]), pltpu.make_async_copy(rflv, rfl, osem.at[1]))
    for store in stores:
        store.start()
    sq[...] = squares
    for d in range(1, NC):
        send(sq, sqr.at[d], qsem.at[d], cs[d], 6)
    left_basis = dot6(left, inverse, nt)
    halves = [red.at[0, 0][pl.ds(h, CH // 2, stride=2), :] for h in (0, 1)]
    own_rf = dot6(jnp.concatenate(halves, axis=1), inverse, nt)
    for d in range(1, NC):
        recv(sqr.at[d], qsem.at[d])
        squares = squares + sqr[d]
    rms = jnp.sqrt(jnp.sum(squares, axis=0, keepdims=True) * (1.0 / n_cols) + EPSILON)
    ownf[...] = own_rf / rms
    basis[...] = left_basis * -(1.0 - MOMENTUM_KEEP)
    update[...] = left_basis * (-scale / rms)
    sent(gram.at[pl.ds(0, 8 * (NC - 1))], 6)
    for store in stores:
        store.wait()


def output_kernel(mom, grad, rfh, rfl, basis, update, ownf, momo, wupd, faco):
    nt = ((1,), (1,))
    high, low = split(update[...])
    rows = jnp.concatenate([basis[...].astype(BF16), high, low], axis=0)
    for first in range(0, HALF, BLK):
        at = slice(first, min(first + BLK, HALF))
        product = dot(rows, rfh[at, :], nt)
        momo[:, at] = mom[:, at] + grad[:, at].astype(F32) + product[:ROWS]
        wupd[:, at] = (product[ROWS:2 * ROWS] + (product[2 * ROWS:] + dot(high, rfl[at, :], nt))).astype(BF16)

    @pl.when(pl.program_id(0) == 0)
    def _():
        faco[...] = ownf[...]


def shards(momentum, gradient, factor):
    rows = momentum.shape[0] * lax.axis_size("row")
    n_cols = momentum.shape[1] * lax.axis_size("col")
    scale = STEP_SIZE * math.sqrt(rows / factor.shape[1])
    dma, vmem, hbm = pltpu.SemaphoreType.DMA, pltpu.VMEM, pl.BlockSpec(memory_space=pl.ANY)
    inside = pl.BlockSpec(memory_space=pltpu.VMEM)
    shape = jax.ShapeDtypeStruct
    flat, natural = vmem((NX, NZ, CH, 128), F32), vmem((NX * NZ * CH, 128), F32)
    gather_sems = [dma((17,)), dma((4, 7)), dma((16,)), dma((4,))]
    rows16 = vmem((NC, ROWS // NC, RANK), F32)
    small = vmem((4, 8, RANK), F32)
    wide, tall, full = vmem((ROWS, COLS), BF16), vmem((COLS, ROWS), BF16), vmem((COLS, RANK), BF16)
    rfh, rfl, basis, update, ownf = pl.pallas_call(
        functools.partial(factor_kernel, n_cols=n_cols, scale=scale),
        out_shape=(
            shape((COLS, RANK), BF16), shape((COLS, RANK), BF16),
            shape((ROWS, RANK), F32), shape((ROWS, RANK), F32), shape((CH // 2, RANK), F32)),
        in_specs=[hbm, hbm, inside],
        out_specs=(hbm, hbm, inside, inside, inside),
        scratch_shapes=[
            vmem((ROWS, COLS), F32), wide, wide, wide, tall, tall, flat, natural, rows16, rows16, rows16,
            natural, flat, flat, natural, vmem((2, 8, 2, CA // 2, 128), F32), vmem((2, 8, 2, CA, 128), F32),
            vmem((2, 9, CA, 128), F32), vmem((2, 2, 9, 2, CB, 128), F32), vmem((4, CB, 128), F32),
            vmem((RANK, RANK), F32), small, small, small, small, vmem((NC, 4, 8, RANK), F32),
            vmem((RANK, RANK), F32), full, full, vmem((8, RANK), F32), vmem((NC, 8, RANK), F32),
            dma((2,)), dma((7,)), dma((1,)), *gather_sems, *gather_sems, dma((2, NC)),
            dma((4, 8)), dma((2, 9)), dma((2, 2, 9)), dma((4,)), dma((5, NC)), dma((NC,)), dma((2,)),
        ],
        compiler_params=pltpu.CompilerParams(collective_id=0, has_side_effects=True, vmem_limit_bytes=60 * 2**20),
        name="right_factor",
    )(momentum, gradient, factor)
    whole = pl.BlockSpec((ROWS, RANK), lambda b: (0, 0))
    across = pl.BlockSpec((ROWS, HALF), lambda b: (0, b))
    down = pl.BlockSpec((HALF, RANK), lambda b: (b, 0))
    chunk = pl.BlockSpec((CH // 2, RANK), lambda b: (0, 0))
    return pl.pallas_call(
        output_kernel,
        grid=(2,),
        out_shape=(shape((ROWS, COLS), F32), shape((ROWS, COLS), BF16), shape((CH // 2, RANK), F32)),
        in_specs=[across, across, down, down, whole, whole, chunk],
        out_specs=(across, across, chunk),
        compiler_params=pltpu.CompilerParams(vmem_limit_bytes=60 * 2**20),
        name="outputs",
    )(momentum, gradient, rfh, rfl, basis, update, ownf)


def solution(mesh):
    placed = (P("row", "col"), P("row", "col"), P(("col", "row"), None))
    return jax.shard_map(shards, mesh=mesh, in_specs=placed, out_specs=placed, check_vma=False)
```

```python
import functools
import math

import jax
import jax.numpy as jnp
from jax import lax
from jax.experimental import pallas as pl
from jax.experimental.pallas import tpu as pltpu
from jax.sharding import PartitionSpec as P

HIGHEST = lax.Precision.HIGHEST
MOMENTUM_KEEP = 0.8
STEP_SIZE = 0.3
EPSILON = 1e-06
F32 = jnp.float32
BF16 = jnp.bfloat16

NX, NZ = 4, 16
NC = 8
CH = 104
CA = 80
CB = CH - CA
ROWS, COLS, RANK = 128, 3328, 256
BLK = 256
NBLK = COLS // BLK
HALF = COLS // 2
NB = 32


def split(value):
    high = value.astype(BF16)
    return high, (value - high.astype(F32)).astype(BF16)


def dot(a, b, dims=((1,), (0,))):
    return lax.dot_general(a, b, (dims, ((), ())), preferred_element_type=F32)


def dot3(a, b, dims=((1,), (0,))):
    return dot(a[0], b[0], dims) + (dot(a[0], b[1], dims) + dot(a[1], b[0], dims))


def dot6(a, b, dims=((1,), (0,))):
    return lax.dot_general(a, b, (dims, ((), ())), precision=HIGHEST, preferred_element_type=F32)


class Links:
    def __init__(self, ssem, rsem):
        self.ssem, self.rsem = ssem, rsem
        self.r, self.c = lax.axis_index("row"), lax.axis_index("col")
        self.x, self.z = self.r // NZ, self.r % NZ

        x, z, c = self.x, self.z, self.c
        self.sign = 1 - 2 * lax.rem(c, 2)
        self.xs = {d: {"row": self.to_x(d) * NZ + z, "col": c} for d in (1, 2, 3)}
        self.zs = {d: {"row": x * NZ + self.to_z(d), "col": c} for d in (1, 4, 5, 8, 11, 12, 15)}
        self.qs = {d: {"row": x * NZ + (z // 4) * 4 + lax.rem(z + d, 4), "col": c} for d in (1, 2, 3)}
        self.cs = {d: {"row": self.r, "col": lax.rem(c + d, NC)} for d in range(1, NC)}

    def to_x(self, d):
        return lax.rem(self.x + self.sign * d + NX, NX)

    def to_z(self, d):
        return lax.rem(self.z + self.sign * d + NZ, NZ)

    def copy(self, src, dst, recv, device, slot=0):
        return pltpu.make_async_remote_copy(
            src_ref=src, dst_ref=dst, send_sem=self.ssem.at[slot], recv_sem=recv,
            device_id=device, device_id_type=pl.DeviceIdType.MESH)

    def send(self, src, dst, recv, device, slot):
        self.copy(src, dst, recv, device, slot).start()

    def recv(self, dst, sem):
        self.copy(dst, dst, sem, self.xs[1]).wait_recv()

    def sent(self, ref, slot):
        self.copy(ref, ref, self.rsem, self.xs[1], slot).wait_send()

    def greet(self, peers):
        barrier = pltpu.get_barrier_semaphore()
        for peer in peers:
            pl.semaphore_signal(barrier, inc=1, device_id=peer, device_id_type=pl.DeviceIdType.MESH)
        return lambda: pl.semaphore_wait(barrier, len(peers))


def block(b):
    return pl.ds(pl.multiple_of(b * BLK, BLK), BLK)


def split_rows(ref, b):
    parts = [split(ref[pl.ds(2 * BLK * b + h, BLK, stride=2), :]) for h in (0, 1)]
    return tuple(jnp.concatenate(p, axis=1) for p in zip(*parts))


SLOT = {0: 0, 1: 1, 15: 2, 5: 3, 11: 4, 2: 5, 14: 6, 6: 7, 10: 8, 4: 9, 12: 10, 7: 11, 9: 12, 3: 13, 13: 14, 8: 15}
GROUPS = ((0, 1), (1, 2), (3, 2), (5, 2), (7, 2), (9, 2), (11, 2), (13, 2), (15, 1))


def gather(t, buf, natural, sems, work, before_b=lambda: None):
    zsem, xsem, bsem, bxsem = sems
    xs, send, recv = t.xs, t.send, t.recv
    right, left, far_right, far_left = t.zs[1], t.zs[15], t.zs[5], t.zs[11]
    half = CA // 2

    def one(k, lo=0, size=CA):
        return buf.at[0, k, pl.ds(lo, size)]

    def four(k):
        return buf.at[pl.ds(0, NX), k, pl.ds(CA, CB)]

    def many(i, g, lo=0, size=CA):
        return buf.at[i, pl.ds(GROUPS[g][0], GROUPS[g][1]), pl.ds(lo, size)]

    def pass_a(k, *ways):
        if k:
            recv(one(k), zsem.at[k])
        for to, device in ways:
            send(one(k), one(to), zsem.at[to], device, 0)

    def pass_b(k, *ways):
        if k:
            recv(four(k), bsem.at[k])
        for to, device in ways:
            send(four(k), four(to), bsem.at[to], device, 0)

    def side(g):
        send(many(0, g), many(1, g), xsem.at[0, g], xs[1], 0)
        send(many(0, g), many(3, g), xsem.at[1, g], xs[3], 0)

    def forward(g):
        recv(many(1, g), xsem.at[0, g])
        send(many(1, g, 0, half), many(2, g, 0, half), xsem.at[2, g], xs[1], 0)
        recv(many(3, g), xsem.at[1, g])
        send(many(3, g, half, half), many(2, g, half, half), xsem.at[3, g], xs[3], 0)

    pass_a(0, (3, far_right), (4, far_left), (1, right), (2, left))
    before_b()
    for d in (1, 2, 3):
        send(buf.at[0, 0, pl.ds(CA, CB)], buf.at[d, 0, pl.ds(CA, CB)], bxsem.at[d], xs[d], 0)
    side(0)
    for d in (1, 2, 3):
        recv(buf.at[d, 0, pl.ds(CA, CB)], bxsem.at[d])
    pass_b(0, (3, far_right), (4, far_left), (1, right), (2, left))
    work(0)
    pass_a(1, (5, right))
    pass_a(2, (6, left))
    side(1)
    forward(0)
    pass_a(3, (7, right), (9, left))
    pass_a(4, (8, left), (10, right))
    side(2)
    pass_b(1, (5, right))
    pass_b(2, (6, left))
    work(1)
    pass_b(3, (7, right), (9, left))
    pass_b(4, (8, left), (10, right))
    forward(1)
    pass_a(5)
    pass_a(6)
    side(3)
    pass_a(7, (11, right))
    pass_a(8, (12, left))
    side(4)
    pass_a(9, (13, left))
    pass_a(10, (14, right))
    side(5)
    forward(2)
    pass_b(5)
    pass_b(6)
    pass_b(7, (11, right))
    pass_b(8, (12, left))
    pass_b(9, (13, left))
    pass_b(10, (14, right))
    work(2)
    forward(3)
    forward(4)
    pass_a(11)
    pass_a(12)
    send(one(11, 0, half), one(15, 0, half), zsem.at[15], right, 0)
    send(one(12, half, half), one(15, half, half), zsem.at[16], left, 0)
    side(6)
    pass_a(13)
    pass_a(14)
    side(7)
    pass_b(11)
    pass_b(12, (15, left))
    forward(5)
    recv(one(15, 0, half), zsem.at[15])
    recv(one(15, half, half), zsem.at[16])
    side(8)
    send(many(0, 8), many(2, 8), xsem.at[2, 8], xs[2], 0)
    pass_b(13)
    pass_b(14)
    work(3)
    forward(6)
    forward(7)
    pass_b(15)
    for i, way in ((1, 0), (3, 1), (2, 2)):
        recv(many(i, 8), xsem.at[way, 8])
    for g in range(len(GROUPS) - 1):
        recv(many(2, g, 0, half), xsem.at[2, g])
        recv(many(2, g, half, half), xsem.at[3, g])
    t.sent(natural.at[pl.ds(0, 6552)], 0)

    for d, k in SLOT.items():
        n = t.to_z(-d)
        for i in range(NX):
            row = t.to_x(-i) * NZ + n
            natural[pl.ds(pl.multiple_of(CH * row, 8), CH), :] = buf[i, k]


def factor_kernel(mom, grad, fac, rfh, rfl, basis, update, ownf,
                  momv, gradv, bhi, blo, th, gat, gat2, ppart, precv, panel,
                  term, part, red, red2, xh, xf, za, zb, xb, gram, g0, g1, g2, g3, g4, aw, rfhv, rflv, sq, sqr,
                  lsem, ssem, tsem, agaz, agax, agbz, agbx, bgaz, bgax, bgbz, bgbx, psem,
                  rsx, rsza, rszb, rsxb, gsem, qsem, osem, *, n_cols, scale):
    t = Links(ssem, psem.at[0, 0])
    t2 = Links(tsem, psem.at[0, 0])
    r, c, x, z = t.r, t.c, t.x, t.z
    xs, zs, qs, cs, send, recv, sent = t.xs, t.zs, t.qs, t.cs, t.send, t.recv, t.sent
    loads = (pltpu.make_async_copy(mom, momv, lsem.at[0]), pltpu.make_async_copy(grad, gradv, lsem.at[1]))
    for load in loads:
        load.start()
    greeted = t.greet([*xs.values(), *zs.values(), *qs.values(), *cs.values()])

    gat.at[0, 0][pl.ds(0, CH // 2, stride=2), :] = fac[:, :128]
    gat.at[0, 0][pl.ds(1, CH // 2, stride=2), :] = fac[:, 128:]
    greeted()

    def prepare(b):
        at = block(b)
        value = momv[:, at] + gradv[:, at].astype(F32)
        high, low = split(value)
        bhi[:, at], blo[:, at] = high, low
        th[at, :ROWS], th[at, ROWS:] = split(value.T)

    def prepare_some(i):
        if i == 0:
            for load in loads:
                load.wait()

        def step(b, carry):
            prepare(b)
            return carry

        lax.fori_loop(*((0, 3), (3, 6), (6, 10), (10, NBLK))[i], step, 0)

    gather(t, gat, gat2, (agaz, agax, agbz, agbx), prepare_some)

    def panel_step(b, total):
        at = block(b)
        return total + dot3((bhi[:, at], blo[:, at]), split_rows(gat2, b))

    total = lax.fori_loop(0, NBLK, panel_step, jnp.zeros((ROWS, RANK), F32))
    ppart[...] = total.reshape(NC, ROWS // NC, RANK)
    for d in range(1, NC):
        send(ppart.at[cs[d]["col"]], precv.at[d], psem.at[0, d], cs[d], 1)
    mine = ppart[c]
    for d in range(1, NC):
        recv(precv.at[d], psem.at[0, d])
        mine = mine + precv[d]
    panel[c] = mine
    for d in range(1, NC):
        send(panel.at[c], panel.at[c], psem.at[1, d], cs[d], 1)
    for d in range(1, NC):
        recv(panel.at[lax.rem(c - d + NC, NC)], psem.at[1, d])
    sent(gat2.at[pl.ds(0, 14 * 32)], 1)

    left = panel[...].reshape(ROWS, RANK)
    gram[...] = dot6(left.T, left)

    def gram_rows(xi):
        return pl.ds(pl.multiple_of(32 * c + 8 * xi, 8), 8)

    for d in (1, 2, 3):
        send(gram.at[gram_rows(t.to_x(d))], g0.at[d], gsem.at[0, d], xs[d], 2)

    def gram_0():
        total = gram[gram_rows(x), :]
        for d in (1, 2, 3):
            recv(g0.at[d], gsem.at[0, d])
            total = total + g0[d]
        g1[0] = total
        for d in (1, 2, 3):
            send(g1.at[0], g1.at[d], gsem.at[1, d], qs[d], 2)

    def gram_1():
        total = g1[0]
        for d in (1, 2, 3):
            recv(g1.at[d], gsem.at[1, d])
            total = total + g1[d]
        g2[0] = total
        for d in (1, 2, 3):
            send(g2.at[0], g2.at[d], gsem.at[2, d], zs[4 * d], 2)

    def gram_2():
        total = g2[0]
        for d in (1, 2, 3):
            recv(g2.at[d], gsem.at[2, d])
            total = total + g2[d]
        g3[x] = total
        for d in (1, 2, 3):
            send(g3.at[x], g3.at[x], gsem.at[3, d], xs[d], 2)

    def gram_3():
        for d in (1, 2, 3):
            recv(g3.at[t.to_x(-d)], gsem.at[3, d])
        g4[c] = g3[...]
        for d in range(1, NC):
            send(g4.at[c], g4.at[c], gsem.at[4, d], cs[d], 3)

    def gram_4():
        for d in range(1, NC):
            recv(g4.at[lax.rem(c - d + NC, NC)], gsem.at[4, d])
        aw[...] = g4[...].reshape(RANK, RANK)
        sent(gram.at[pl.ds(0, 96)], 2)
        sent(g4.at[pl.ds(0, NC - 1)], 3)

    sub = lax.broadcasted_iota(jnp.int32, (NB, 128), 0)
    lane = lax.broadcasted_iota(jnp.int32, (NB, 128), 1)
    sub_w = lax.broadcasted_iota(jnp.int32, (NB, RANK), 0)
    lane_w = lax.broadcasted_iota(jnp.int32, (NB, RANK), 1)
    i_all = lax.broadcasted_iota(jnp.int32, (RANK, RANK), 0)
    j_all = lax.broadcasted_iota(jnp.int32, (RANK, RANK), 1)

    def factor_block(k):
        first = pl.multiple_of(NB * k, NB)
        rows = aw[pl.ds(first, NB), :]
        near = jnp.where(k < 4, rows[:, :128], rows[:, 128:])
        near = pltpu.roll(near, lax.rem(128 - NB * lax.rem(k, 4), 128), 1)
        e = jnp.where(lane < NB, near, jnp.where(lane - NB == sub, 1.0, 0.0))
        for j in range(0, NB, 4):
            cols = [jnp.broadcast_to(e[:, j + i:j + i + 1], (NB, 128)) for i in range(4)]
            pivots = [e[j + i:j + i + 1, :] for i in range(4)]
            for i in range(4):
                at = slice(j + i, j + i + 1)
                ratio = jnp.where(sub > j + i, cols[i] * (1.0 / cols[i][at, :]), 0.0)
                for m in range(i + 1, 4):
                    cols[m] = cols[m] - ratio * cols[m][at, :]
                    pivots[m] = pivots[m] - ratio[j + m:j + m + 1, :] * pivots[i]
                e = e - ratio * pivots[i]
        diagonal = jnp.sum(jnp.where(lane == sub, e, 0.0), axis=1, keepdims=True)
        inverse = (e * (1.0 / jnp.sqrt(diagonal)))[:, NB:2 * NB]
        here = (lane_w >= first) & (lane_w < first + NB)
        rows = jnp.where(here, jnp.where(lane_w - first == sub_w, 1.0, 0.0), rows)
        rows = dot6(inverse, rows)
        below = jnp.where(lane_w >= first + NB, rows, 0.0)
        done = (i_all >= first + NB) & (j_all >= first) & (j_all < first + NB)
        aw[...] = jnp.where(done, 0.0, aw[...]) - dot6(below.T, rows)
        aw[pl.ds(first, NB), :] = rows

    lp_high, lp_low = split(left)
    lp_twice = jnp.concatenate([lp_high, lp_high], axis=0)

    def term_step(b, carry):
        h = dot(th[block(b), :], lp_twice) + dot(th[block(b), :ROWS], lp_low)
        term[pl.ds(2 * BLK * b, BLK, stride=2), :] = h[:, :128]
        term[pl.ds(2 * BLK * b + 1, BLK, stride=2), :] = h[:, 128:]
        pl.when(b == 6)(gram_0)
        return carry

    lax.fori_loop(0, NBLK, term_step, 0)
    gram_1()

    def place(k, carry):
        n = t.to_z(jnp.where(k == 15, 0, jnp.where(lax.rem(k, 2) == 0, 8 - k // 2, k // 2 - 7)))
        for i in range(NX):
            row = t.to_x(i) * NZ + n
            part[i, k] = term[pl.ds(pl.multiple_of(CH * row, 8), CH), :]
        return carry

    lax.fori_loop(0, NZ, place, 0)

    half = CA // 2

    def pair(i, s, lo=0, size=CA):
        return part.at[i, pl.ds(2 * s, 2), pl.ds(lo, size)]

    def send_half(s):
        send(pair(2, s, 0, half), xh.at[0, s], rsx.at[0, s], xs[1], 4)
        send(pair(2, s, half, half), xh.at[1, s], rsx.at[1, s], xs[3], 4)

    def send_full(s):
        two = pl.ds(2 * s, 2)
        recv(xh.at[0, s], rsx.at[0, s])
        part[1, two, :half, :] += xh[0, s]
        send(pair(1, s), xf.at[0, s], rsx.at[2, s], xs[1], 4)
        recv(xh.at[1, s], rsx.at[1, s])
        part[3, two, half:CA, :] += xh[1, s]
        send(pair(3, s), xf.at[1, s], rsx.at[3, s], xs[3], 4)

    def take_full(s):
        two = pl.ds(2 * s, 2)
        recv(xf.at[0, s], rsx.at[2, s])
        recv(xf.at[1, s], rsx.at[3, s])
        part[0, two, :CA, :] += xf[0, s] + xf[1, s]

    send_half(0)
    send_half(1)
    send_full(0)

    def reduce_step(s, carry):
        @pl.when(s < 6)
        def _():
            send_half(s + 2)

        for i, g in enumerate((1, 0)):
            rows = pl.ds(2 * g, 2)
            kl, kr = jnp.maximum(2 * s - 1, 0), 2 * s + 2

            @pl.when(s > 0)
            def _():
                recv(zb.at[1, i, s], rszb.at[1, i, s])
                part[rows, kl, CA:, :] += zb[1, i, s]

            send(part.at[rows, kl, pl.ds(CA, CB)], zb.at[1, i, s + 1], rszb.at[1, i, s + 1], zs[15], 4)

            @pl.when(s < 7)
            def _():
                @pl.when(s > 0)
                def _():
                    recv(zb.at[0, i, s], rszb.at[0, i, s])
                    part[rows, kr, CA:, :] += zb[0, i, s]

                send(part.at[rows, kr, pl.ds(CA, CB)], zb.at[0, i, s + 1], rszb.at[0, i, s + 1], zs[1], 4)

        @pl.when(s < 7)
        def _():
            send_full(s + 1)

        take_full(s)

        @pl.when(s > 0)
        def _():
            recv(za.at[0, s], rsza.at[0, s])
            part[0, 2 * s, :CA, :] += za[0, s]

        send(part.at[0, 2 * s, pl.ds(0, CA)], za.at[0, s + 1], rsza.at[0, s + 1], zs[1], 4)

        @pl.when(s < 7)
        def _():
            @pl.when(s > 0)
            def _():
                recv(za.at[1, s], rsza.at[1, s])
                part[0, 2 * s + 1, :CA, :] += za[1, s]

            send(part.at[0, 2 * s + 1, pl.ds(0, CA)], za.at[1, s + 1], rsza.at[1, s + 1], zs[15], 4)

        for when, stage in enumerate((gram_2, gram_3, gram_4)):
            pl.when(s == when)(stage)

        @pl.when(s > 2)
        def _():
            factor_block(s - 3)

        return carry

    lax.fori_loop(0, 8, reduce_step, 0)
    for i, g in enumerate((1, 0)):
        recv(zb.at[1, i, 8], rszb.at[1, i, 8])
        recv(zb.at[0, i, 7], rszb.at[0, i, 7])
        part[2 * g:2 * g + 2, 15, CA:, :] += zb[1, i, 8] + zb[0, i, 7]
    for d in (1, 2, 3):
        send(part.at[d, 15, pl.ds(CA, CB)], xb.at[d], rsxb.at[d], xs[d], 4)
    recv(za.at[0, 8], rsza.at[0, 8])
    recv(za.at[1, 7], rsza.at[1, 7])
    red[0, 0, :CA, :] = part[0, 15, :CA, :] + (za[0, 8] + za[1, 7])

    def finish_b():
        total = part[0, 15, CA:, :]
        for d in (1, 2, 3):
            recv(xb.at[d], rsxb.at[d])
            total = total + xb[d]
        red[0, 0, CA:, :] = total

    def factor_rest(i):
        if i:
            factor_block(jnp.int32(i + 4))

    gather(t2, red, red2, (bgaz, bgax, bgbz, bgbx), factor_rest, finish_b)
    sent(term.at[pl.ds(0, 6552)], 4)

    inverse = jnp.where(i_all >= j_all, aw[...], 0.0)
    nt = ((1,), (1,))
    inv = split(inverse)

    def right_step(b, squares):
        rf = dot3(split_rows(red2, b), inv, nt)
        rfhv[block(b), :], rflv[block(b), :] = split(rf)
        return squares + jnp.sum((rf * rf).reshape(BLK // 8, 8, RANK), axis=0)

    squares = lax.fori_loop(0, NBLK, right_step, jnp.zeros((8, RANK), F32))
    stores = (pltpu.make_async_copy(rfhv, rfh, osem.at[0]), pltpu.make_async_copy(rflv, rfl, osem.at[1]))
    for store in stores:
        store.start()
    sq[...] = squares
    for d in range(1, NC):
        send(sq, sqr.at[d], qsem.at[d], cs[d], 6)
    left_basis = dot6(left, inverse, nt)
    halves = [red.at[0, 0][pl.ds(h, CH // 2, stride=2), :] for h in (0, 1)]
    own_rf = dot6(jnp.concatenate(halves, axis=1), inverse, nt)
    for d in range(1, NC):
        recv(sqr.at[d], qsem.at[d])
        squares = squares + sqr[d]
    rms = jnp.sqrt(jnp.sum(squares, axis=0, keepdims=True) * (1.0 / n_cols) + EPSILON)
    ownf[...] = own_rf / rms
    basis[...] = left_basis * -(1.0 - MOMENTUM_KEEP)
    update[...] = left_basis * (-scale / rms)
    sent(gram.at[pl.ds(0, 8 * (NC - 1))], 6)
    for store in stores:
        store.wait()


def output_kernel(mom, grad, rfh, rfl, basis, update, ownf, momo, wupd, faco):
    nt = ((1,), (1,))
    high, low = split(update[...])
    rows = jnp.concatenate([basis[...].astype(BF16), high, low], axis=0)
    for first in range(0, HALF, BLK):
        at = slice(first, min(first + BLK, HALF))
        product = dot(rows, rfh[at, :], nt)
        momo[:, at] = mom[:, at] + grad[:, at].astype(F32) + product[:ROWS]
        wupd[:, at] = (product[ROWS:2 * ROWS] + (product[2 * ROWS:] + dot(high, rfl[at, :], nt))).astype(BF16)

    @pl.when(pl.program_id(0) == 0)
    def _():
        faco[...] = ownf[...]


def shards(momentum, gradient, factor):
    rows = momentum.shape[0] * lax.axis_size("row")
    n_cols = momentum.shape[1] * lax.axis_size("col")
    scale = STEP_SIZE * math.sqrt(rows / factor.shape[1])
    dma, vmem, hbm = pltpu.SemaphoreType.DMA, pltpu.VMEM, pl.BlockSpec(memory_space=pl.ANY)
    inside = pl.BlockSpec(memory_space=pltpu.VMEM)
    shape = jax.ShapeDtypeStruct
    flat, natural = vmem((NX, NZ, CH, 128), F32), vmem((NX * NZ * CH, 128), F32)
    gather_sems = [dma((17,)), dma((4, 9)), dma((16,)), dma((4,))]
    rows16 = vmem((NC, ROWS // NC, RANK), F32)
    small = vmem((4, 8, RANK), F32)
    wide, tall, full = vmem((ROWS, COLS), BF16), vmem((COLS, 2 * ROWS), BF16), vmem((COLS, RANK), BF16)
    rfh, rfl, basis, update, ownf = pl.pallas_call(
        functools.partial(factor_kernel, n_cols=n_cols, scale=scale),
        out_shape=(
            shape((COLS, RANK), BF16), shape((COLS, RANK), BF16),
            shape((ROWS, RANK), F32), shape((ROWS, RANK), F32), shape((CH // 2, RANK), F32)),
        in_specs=[hbm, hbm, inside],
        out_specs=(hbm, hbm, inside, inside, inside),
        scratch_shapes=[
            vmem((ROWS, COLS), F32), wide, wide, wide, tall, flat, natural, rows16, rows16, rows16,
            natural, flat, flat, natural, vmem((2, 8, 2, CA // 2, 128), F32), vmem((2, 8, 2, CA, 128), F32),
            vmem((2, 9, CA, 128), F32), vmem((2, 2, 9, 2, CB, 128), F32), vmem((4, CB, 128), F32),
            vmem((RANK, RANK), F32), small, small, small, small, vmem((NC, 4, 8, RANK), F32),
            vmem((RANK, RANK), F32), full, full, vmem((8, RANK), F32), vmem((NC, 8, RANK), F32),
            dma((2,)), dma((7,)), dma((1,)), *gather_sems, *gather_sems, dma((2, NC)),
            dma((4, 8)), dma((2, 9)), dma((2, 2, 9)), dma((4,)), dma((5, NC)), dma((NC,)), dma((2,)),
        ],
        compiler_params=pltpu.CompilerParams(collective_id=0, has_side_effects=True, vmem_limit_bytes=60 * 2**20),
        name="right_factor",
    )(momentum, gradient, factor)
    whole = pl.BlockSpec((ROWS, RANK), lambda b: (0, 0))
    across = pl.BlockSpec((ROWS, HALF), lambda b: (0, b))
    down = pl.BlockSpec((HALF, RANK), lambda b: (b, 0))
    chunk = pl.BlockSpec((CH // 2, RANK), lambda b: (0, 0))
    return pl.pallas_call(
        output_kernel,
        grid=(2,),
        out_shape=(shape((ROWS, COLS), F32), shape((ROWS, COLS), BF16), shape((CH // 2, RANK), F32)),
        in_specs=[across, across, down, down, whole, whole, chunk],
        out_specs=(across, across, chunk),
        compiler_params=pltpu.CompilerParams(vmem_limit_bytes=60 * 2**20),
        name="outputs",
    )(momentum, gradient, rfh, rfl, basis, update, ownf)


def solution(mesh):
    placed = (P("row", "col"), P("row", "col"), P(("col", "row"), None))
    return jax.shard_map(shards, mesh=mesh, in_specs=placed, out_specs=placed, check_vma=False)
```
